128 devices in a mesh: node: 4 (over z), local: 16 (over x, y), tp: 2 (over core).
Axes of the slice: x: 4, y: 4, z: 4, core: 2. Of those that a mesh axis runs over, the one named last changes fastest.
Arguments:
- mixer_out: bfloat16 [8192, 8192], P(('node', 'local'), 'tp'), may hold values from -6 to 6
- out_proj: bfloat16 [8192, 8192], P('tp', 'local'), may hold values from -0.0625 to 0.0625
- residual: bfloat16 [8192, 8192], P(('node', 'tp'), 'local'), may hold values from -6 to 6
- norm_gain: float32 [8192], replicated, may hold values from 0.1 to 1.9
- router_weight: bfloat16 [8192, 16], replicated, may hold values from -0.0625 to 0.0625
- expert_ids: int32 [8192, 2], P(('node', 'tp')), may hold values from 0 to 15, as said below
- expert_gate: bfloat16 [4, 8192, 12288], P('node', None, ('local', 'tp')), may hold values from -0.0625 to 0.0625
- expert_up: bfloat16 [4, 8192, 12288], P('node', None, ('local', 'tp')), may hold values from -0.0625 to 0.0625
- expert_down: bfloat16 [4, 12288, 8192], P('node', ('local', 'tp')), may hold values from -0.4375 to 0.4375
Outputs:
- layer_out: bfloat16 [8192, 8192], P(('node', 'tp'), 'local')
The draws below stay inside these ranges and needn't reach their ends.
Inputs may be any that keep to these rules, and one draw needn't show every extreme that they name: `expert_ids`: the ids of a row differ. A row names at most one of the experts 0 to 3, and only in its first column. In every aligned block of 1024 rows (the tokens of one (node, tp) group) each of these experts is named by at most 64 rows, and one of them, the same in every block of a draw, by exactly 64 rows.
All inputs are finite; a program needn't handle non-finite values.
Results may differ from the reference program's by a relative error of at most 0.009.
Values may be sent and summed in bfloat16 or wider, within the bound.
No kernel may reach another device: no remote copies, remote signals or barrier semaphores. Data moves between devices by JAX's collectives and lax.ppermute only.
A program may use at most 192 MiB of HBM per device.

```python
import jax
import jax.numpy as jnp
from jax import lax

D = 8192
EXPERTS = 16
DI = 8192
FF = 12288
TOKENS = 8192
TOK_HALF = 1024
CAP = 64
EXP_FLIGHT = 4
N_NODE = 4
N_LOCAL = 16
N_TP = 2


def draw_expert_ids(key, part):
    key = jax.random.fold_in(key, 11)
    groups = TOKENS // TOK_HALF
    keys = jax.random.split(key, 5)
    hottest = jax.random.randint(keys[0], (), 0, EXP_FLIGHT)
    counts = jax.random.randint(keys[1], (groups, EXP_FLIGHT), CAP // 8, CAP // 2 + 1)
    counts = jnp.where(jnp.arange(EXP_FLIGHT)[None, :] == hottest, CAP, counts).astype(jnp.int32)
    starts = jnp.cumsum(counts, axis=1) - counts
    places = jnp.arange(TOK_HALF, dtype=jnp.int32)
    inside = (places[None, :, None] >= starts[:, None, :]) & (places[None, :, None] < (starts + counts)[:, None, :])
    owner = jnp.sum(inside.astype(jnp.int32) * jnp.arange(EXP_FLIGHT, dtype=jnp.int32)[None, None, :], axis=2)
    owned = jnp.any(inside, axis=2)
    spare = EXPERTS - EXP_FLIGHT
    first_other = jax.random.randint(keys[2], (groups, TOK_HALF), 0, spare)
    second_other = (first_other + jax.random.randint(keys[3], (groups, TOK_HALF), 1, spare)) % spare
    first = jnp.where(owned, owner, first_other + EXP_FLIGHT)
    second = second_other + EXP_FLIGHT
    orders = jax.vmap(lambda k: jax.random.permutation(k, TOK_HALF))(jax.random.split(keys[4], groups))
    first = jnp.take_along_axis(first, orders, axis=1)
    second = jnp.take_along_axis(second, orders, axis=1)
    return jnp.stack([first, second], axis=2).reshape(TOKENS, 2).astype(jnp.int32)


def spiked(drawn, stream_key, source, target, shards_of, factor):
    owner, partner = [(jnp.arange(drawn.shape[axis_at]) // (drawn.shape[axis_at] // shards_of)).reshape([-1 if axis == axis_at else 1 for axis in range(drawn.ndim)]) for axis_at in (source, target)]
    chosen = jax.random.permutation(stream_key, shards_of)[partner]
    strong = (owner == chosen) | (owner == (partner + shards_of // 2) % shards_of)
    return jnp.where(strong, factor * drawn, drawn)


def level_of(own_key, shape, shards, least, top_value):
    gain = 1.0
    for axis_at, parts in shards:
        heights = jax.random.uniform(jax.random.fold_in(jax.random.fold_in(own_key, 6), axis_at), (parts,), jnp.float32, least / len(shards), top_value / len(shards))
        gain = gain * jnp.repeat(jnp.exp(heights), shape[axis_at] // parts).reshape((-1,) + (1,) * (len(shape) - 1 - axis_at))
    return gain


def centred(own_key, extent, spread, limit, cuts=(), held_as=jnp.bfloat16):
    entries = spread * jax.random.normal(own_key, extent, jnp.float32)
    if cuts:
        entries = entries * level_of(own_key, extent, cuts, -0.22, 0.18)
    return jnp.clip(entries, -limit, limit).astype(held_as)


def gaussian_with(key, dims, scale, most, cuts, heavy, held_as=jnp.bfloat16):
    drawn = scale * jax.random.normal(key, dims, jnp.float32)
    if cuts:
        drawn = drawn * level_of(key, dims, cuts, -0.22, 0.18)
    return jnp.clip(spiked(drawn, jax.random.fold_in(key, 3), *heavy), -most, most).astype(held_as)


def setup_inputs(seed: int = 0) -> dict:
    seeds = jax.random.split(jax.random.key(seed), 10)
    return {
        "mixer_out": centred(seeds[0], (TOKENS, DI), 1.0, 6.0, ((0, 64), (1, 2))),
        "out_proj": centred(seeds[1], (DI, D), DI ** -0.5, 0.0625, ((0, 2), (1, 16))),
        "residual": centred(seeds[2], (TOKENS, D), 1.0, 6.0, ((0, 8), (1, 16))),
        "norm_gain": jnp.clip(1.0 + 0.18 * jax.random.normal(seeds[3], (D,), jnp.float32), 0.1, 1.9),
        "router_weight": centred(seeds[4], (D, EXPERTS), D ** -0.5, 0.0625),
        "expert_ids": draw_expert_ids(jax.random.fold_in(seeds[9], 71), 0),
        "expert_gate": centred(seeds[6], (EXP_FLIGHT, D, FF), D ** -0.5, 0.0625, ((0, 4), (2, 32))),
        "expert_up": centred(seeds[7], (EXP_FLIGHT, D, FF), D ** -0.5, 0.0625, ((0, 4), (2, 32))),
        "expert_down": gaussian_with(seeds[8], (EXP_FLIGHT, FF, D), (FF // 16) ** -0.5, 0.4375, ((0, 4), (1, 32)), (1, 2, 32, 2.75)),
    }


def reference(mixer_out, out_proj, residual, norm_gain, router_weight, expert_ids, expert_gate, expert_up, expert_down):
    mixed = jnp.dot(mixer_out, out_proj, preferred_element_type=jnp.float32)
    stream = residual.astype(jnp.float32) + mixed
    stream_low = stream.astype(jnp.bfloat16).astype(jnp.float32)
    scale = lax.rsqrt(lax.optimization_barrier(jnp.mean(stream_low * stream_low, axis=1, keepdims=True)) + 1e-06)
    normed = (stream_low * scale * norm_gain[None, :]).astype(jnp.bfloat16)
    logits = jnp.dot(normed, router_weight, preferred_element_type=jnp.float32)
    blocks = N_LOCAL * N_TP
    width = FF // blocks
    row_most = N_NODE * N_TP * CAP
    partner = jnp.where(expert_ids[:, 0] < N_NODE, expert_ids[:, 1], expert_ids[:, 0]).astype(jnp.int32)
    total = jnp.zeros((TOKENS, D), jnp.float32)
    for expert in range(EXP_FLIGHT):
        chosen = jnp.any(expert_ids == expert, axis=1)
        order = jnp.argsort(1 - chosen.astype(jnp.int32), stable=True)[:row_most].astype(jnp.int32)
        valid = chosen[order]
        rows = normed[order]
        row_logits = logits[order]
        other = jnp.take_along_axis(row_logits, partner[order][:, None], axis=1)
        weight = jax.nn.sigmoid(row_logits[:, expert:expert + 1] - other)
        gate = jnp.dot(rows, expert_gate[expert], preferred_element_type=jnp.float32)
        upper = jnp.dot(rows, expert_up[expert], preferred_element_type=jnp.float32)
        hidden = (jax.nn.silu(gate) * upper).astype(jnp.bfloat16)
        hidden_blocks = hidden.reshape(row_most, blocks, width).transpose(1, 0, 2)
        down_blocks = expert_down[expert].reshape(blocks, width, D)

        def add_block(carry, pair):
            piece, weights_block = pair
            part = weight * jnp.dot(piece, weights_block, preferred_element_type=jnp.float32)
            part = lax.optimization_barrier(part.astype(jnp.bfloat16)).astype(jnp.float32)
            return (carry + part, None)
        summed, unused = lax.scan(add_block, jnp.zeros((row_most, D), jnp.float32), (hidden_blocks, down_blocks))
        total = total.at[order].add(jnp.where(valid[:, None], summed, jnp.float32(0.0)))
    return (stream + total).astype(jnp.bfloat16)
```

```python
import jax
import jax.numpy as jnp
from jax import lax
from jax.experimental import pallas as pl
from jax.experimental.pallas import tpu as pltpu
from jax.sharding import PartitionSpec as P

CHUNKS = 4
SIDE = 4


def shift_node(value, by):
    return lax.ppermute(value, "node", [(i, (i + by) % SIDE) for i in range(SIDE)])


def shift_local(value, dx, dy):
    pairs = [
        (x * SIDE + y, ((x + dx) % SIDE) * SIDE + (y + dy) % SIDE)
        for x in range(SIDE)
        for y in range(SIDE)
    ]
    return lax.ppermute(value, "local", pairs)


def swap_core(value):
    return lax.ppermute(value, "tp", [(0, 1), (1, 0)])


def expert_kernel(
    order,
    rows,
    gain,
    router,
    select,
    gate_a,
    gate_b,
    up_a,
    up_b,
    down_a0,
    down_b0,
    down_a1,
    down_b1,
    out,
    acc,
    logit_acc,
    square_acc,
    hidden,
    weight,
    *,
    first_steps,
    width,
    features,
):
    step = pl.program_id(0)
    row_count, block = rows.shape[1], rows.shape[2]

    @pl.when(step == 0)
    def _():
        acc[...] = jnp.zeros_like(acc)
        logit_acc[...] = jnp.zeros_like(logit_acc)
        square_acc[...] = jnp.zeros_like(square_acc)

    @pl.when(step < first_steps)
    def _():
        for part in range(rows.shape[0]):
            span = pl.ds(part * block, block)
            values = rows[part].astype(jnp.float32)
            squares = values * values
            for lane in range(0, block, 128):
                square_acc[...] += squares[:, lane : lane + 128]
            scaled = (values * gain[:, span]).astype(jnp.bfloat16)
            for at, ref in enumerate((gate_a, gate_b, up_a, up_b)):
                acc[at] += jnp.dot(scaled, ref[0, span, :], preferred_element_type=jnp.float32)
            logit_acc[...] += jnp.dot(
                scaled, router[span, :], preferred_element_type=jnp.float32
            )

    @pl.when(step == first_steps - 1)
    def _():
        mean = jnp.sum(square_acc[...], axis=1, keepdims=True) / features
        scale = lax.rsqrt(mean + 1e-06)
        gap = jnp.sum(logit_acc[...] * select[...], axis=1, keepdims=True) * scale
        weight[...] = jnp.broadcast_to(1.0 / (1.0 + jnp.exp(-gap)), weight.shape)
        for core in range(2):
            gate = acc[core] * scale
            upper = acc[2 + core] * scale
            hidden[core] = (gate / (1.0 + jnp.exp(-gate)) * upper).astype(jnp.bfloat16)

    @pl.when(step >= first_steps)
    def _():
        for part, (ref_a, ref_b) in enumerate(((down_a0, down_b0), (down_a1, down_b1))):
            term = jnp.dot(hidden[0], ref_a[0], preferred_element_type=jnp.float32)
            term += jnp.dot(hidden[1], ref_b[0], preferred_element_type=jnp.float32)
            out[part] = (term * weight[:, :1]).astype(jnp.bfloat16)


def run_experts(rows, gain, router, select, order, gate, gate_o, up, up_o, down, down_o):
    blocks, row_count, block = rows.shape
    features, width = gate.shape[1], gate.shape[2]
    per = 2
    first_steps = blocks // per
    grid = (2 * first_steps,)
    head = lambda i: jnp.minimum(i, first_steps - 1)
    tail = lambda i: jnp.maximum(i - first_steps, 0)
    wide = pl.BlockSpec((1, per * block, width), lambda i, order: (0, head(i), 0))

    def down_spec(part):
        return pl.BlockSpec(
            (1, width, block), lambda i, order: (0, 0, order[tail(i) * per + part])
        )

    return pl.pallas_call(
        lambda *refs: expert_kernel(
            *refs, first_steps=first_steps, width=width, features=features
        ),
        out_shape=jax.ShapeDtypeStruct((blocks, row_count, block), jnp.bfloat16),
        grid_spec=pltpu.PrefetchScalarGridSpec(
            num_scalar_prefetch=1,
            grid=grid,
            in_specs=[
                pl.BlockSpec((per, row_count, block), lambda i, order: (head(i), 0, 0)),
                pl.BlockSpec((1, per * block), lambda i, order: (0, head(i))),
                pl.BlockSpec((per * block, router.shape[1]), lambda i, order: (head(i), 0)),
                pl.BlockSpec((row_count, router.shape[1]), lambda i, order: (0, 0)),
                wide,
                wide,
                wide,
                wide,
                down_spec(0),
                down_spec(0),
                down_spec(1),
                down_spec(1),
            ],
            out_specs=pl.BlockSpec((per, row_count, block), lambda i, order: (tail(i), 0, 0)),
            scratch_shapes=[
                pltpu.VMEM((4, row_count, width), jnp.float32),
                pltpu.VMEM((row_count, router.shape[1]), jnp.float32),
                pltpu.VMEM((row_count, 128), jnp.float32),
                pltpu.VMEM((2, row_count, width), jnp.bfloat16),
                pltpu.VMEM((row_count, 128), jnp.float32),
            ],
        ),
        compiler_params=pltpu.CompilerParams(
            dimension_semantics=("arbitrary",), vmem_limit_bytes=40 * 1024 * 1024
        ),
        cost_estimate=pl.CostEstimate(
            flops=2 * row_count * features * width * 6,
            bytes_accessed=features * width * 12 + 4 * blocks * row_count * block,
            transcendentals=0,
        ),
    )(order, rows, gain, router, select, gate, gate_o, up, up_o, down, down_o, down, down_o)


def plane_sum(spread):
    rows = spread.shape[2]
    half = rows // 2
    f32 = jnp.float32
    low, high = spread[:, :, :half], spread[:, :, half:]
    low_in = [shift_local(low[d], d, 0) for d in (1, 3, 2)]
    high_in = [shift_local(high[:, d], 0, d) for d in (1, 3, 2)]
    low = sum((v.astype(f32) for v in low_in), low[0].astype(f32)).astype(jnp.bfloat16)
    high = sum((v.astype(f32) for v in high_in), high[:, 0].astype(f32)).astype(jnp.bfloat16)
    low_in = [shift_local(low[d], 0, d) for d in (1, 3, 2)]
    high_in = [shift_local(high[d], d, 0) for d in (1, 3, 2)]
    low = sum((v.astype(f32) for v in low_in), low[0].astype(f32)).astype(jnp.bfloat16)
    high = sum((v.astype(f32) for v in high_in), high[0].astype(f32)).astype(jnp.bfloat16)
    return jnp.concatenate([low, high], axis=0)


def body(
    mixer_out,
    out_proj,
    residual,
    norm_gain,
    router_weight,
    expert_ids,
    expert_gate,
    expert_up,
    expert_down,
):
    f32 = jnp.float32
    node = lax.axis_index("node")
    local = lax.axis_index("local")
    core = lax.axis_index("tp")
    half_rows, col_width = residual.shape
    capacity = half_rows // 16
    spots = SIDE * capacity
    gate_o, up_o, down_o = (swap_core(w) for w in (expert_gate, expert_up, expert_down))

    first, partner = expert_ids[:, 0], expert_ids[:, 1]
    routed = first < SIDE
    relative = lax.rem(first - node + SIDE, SIDE)
    marks = (routed[:, None] & (relative[:, None] == jnp.arange(SIDE)[None, :])).astype(jnp.int32)
    slots = jnp.sum((jnp.cumsum(marks, axis=0) - marks) * marks, axis=1)
    spot = jnp.where(routed, relative * capacity + slots, -1)
    picked = spot[None, :] == jnp.arange(spots)[:, None]
    placed = (spot[:, None] == jnp.arange(spots)[None, :]).astype(jnp.bfloat16)
    partners = jnp.sum(jnp.where(picked, partner[None, :], 0), axis=1).reshape(SIDE, capacity)
    partners = jnp.concatenate(
        [partners[0]] + [shift_node(partners[d], d) for d in range(1, SIDE)], axis=0
    )
    experts = jnp.arange(router_weight.shape[1])[None, :]
    select = (experts == node).astype(f32) - (experts == partners[:, None]).astype(f32)
    picked = picked.astype(jnp.bfloat16)

    rows = mixer_out.shape[0] // CHUNKS
    streams = []
    for j in range(CHUNKS):
        full = lax.all_gather(mixer_out[j * rows : (j + 1) * rows], "local", axis=0, tiled=True)
        half = full.shape[0] // 2
        theirs = lax.dynamic_slice_in_dim(full, (1 - core) * half, half, 0)
        mine = lax.dynamic_slice_in_dim(full, core * half, half, 0)
        sent = swap_core(jnp.dot(theirs, out_proj, preferred_element_type=f32))
        kept = jnp.dot(mine, out_proj, preferred_element_type=f32)
        part = residual.reshape(-1, CHUNKS, rows, col_width)[:, j].astype(f32)
        streams.append(part + (kept + sent).reshape(part.shape))
    stream = jnp.stack(streams, axis=1).reshape(half_rows, col_width)
    stream_low = stream.astype(jnp.bfloat16)
    bucket = (
        jnp.dot(picked, stream_low, preferred_element_type=f32)
        .astype(jnp.bfloat16)
        .reshape(SIDE, capacity, col_width)
    )
    landed = jnp.concatenate(
        [bucket[0]] + [shift_node(bucket[d], d) for d in range(1, SIDE)], axis=0
    )
    gathered = lax.all_gather(landed, "local", axis=0, tiled=False)
    x, y = local // SIDE, local % SIDE
    ahead = jnp.arange(SIDE)
    order = (
        ((x + ahead) % SIDE)[:, None] * SIDE + ((y + ahead) % SIDE)[None, :]
    ).reshape(-1).astype(jnp.int32)
    spread = run_experts(
        gathered,
        norm_gain[None, :],
        router_weight,
        select,
        order,
        expert_gate,
        gate_o,
        expert_up,
        up_o,
        expert_down,
        down_o,
    )
    summed = plane_sum(spread.reshape(SIDE, SIDE, spots, col_width))
    summed = summed.reshape(SIDE, capacity, col_width)
    returned = jnp.concatenate(
        [summed[0]] + [shift_node(summed[d], -d) for d in range(1, SIDE)], axis=0
    )
    expert_sum = jnp.dot(placed, returned, preferred_element_type=f32)
    return (stream + expert_sum).astype(jnp.bfloat16)


def solution(mesh):
    placed = (
        P(("node", "local"), "tp"),
        P("tp", "local"),
        P(("node", "tp"), "local"),
        P(),
        P(),
        P(("node", "tp"), None),
        P("node", None, ("local", "tp")),
        P("node", None, ("local", "tp")),
        P("node", ("local", "tp"), None),
    )
    return jax.shard_map(
        body, mesh=mesh, in_specs=placed, out_specs=P(("node", "tp"), "local"), check_vma=False
    )
```

```python
import jax
import jax.numpy as jnp
from jax import lax
from jax.experimental import pallas as pl
from jax.experimental.pallas import tpu as pltpu
from jax.sharding import PartitionSpec as P

SIDE = 4
PER = 1
VMEM = 56 * 1024 * 1024
F32 = jnp.float32
BF16 = jnp.bfloat16


def shift_node(value, by):
    return lax.ppermute(value, "node", [(i, (i + by) % SIDE) for i in range(SIDE)])


def shift(value, axis, by):
    dx, dy = (by, 0) if axis == "x" else (0, by)
    pairs = [
        (x * SIDE + y, ((x + dx) % SIDE) * SIDE + (y + dy) % SIDE)
        for x in range(SIDE)
        for y in range(SIDE)
    ]
    return lax.ppermute(value, "local", pairs)


def shift_mixed(value, far, by):
    pairs = []
    for x in range(SIDE):
        for y in range(SIDE):
            for core in range(2):
                dx, dy = (by, 0) if (core == 0) != far else (0, by)
                to = ((x + dx) % SIDE) * SIDE + (y + dy) % SIDE
                pairs.append(((x * SIDE + y) * 2 + core, to * 2 + core))
    return lax.ppermute(value, ("local", "tp"), pairs)


def swap_core(value):
    return lax.ppermute(value, "tp", [(0, 1), (1, 0)])


def roll_to(value, by, axis):
    doubled = jnp.concatenate([value, value], axis=axis)
    return lax.dynamic_slice_in_dim(doubled, by, value.shape[axis], axis)


def ring(value, axis):
    half = value.shape[0] // 2
    behind = shift(value, axis, 1)
    ahead = shift(value, axis, -1)
    across = [shift(behind[:half], axis, 1), shift(ahead[half:], axis, -1)]
    return ahead, across, behind


def products_kernel(order, rows, *refs, first, last, features):
    weights, refs = [refs[2 * b : 2 * b + 2] for b in range(PER)], refs[2 * PER :]
    routers, refs = refs[:PER], refs[PER:]
    gains, refs = refs[:PER], refs[PER:]
    carried = None
    if not first:
        carried, refs = refs[:3], refs[3:]
    if last:
        select, hidden, weight, acc, logits, squares = refs
    else:
        acc, logits, squares = refs

    @pl.when(pl.program_id(0) == 0)
    def _():
        for at, ref in enumerate((acc, logits, squares)):
            ref[...] = jnp.zeros_like(ref) if first else carried[at][...]

    scaled = []
    for b in range(PER):
        values = rows[b].astype(F32)
        square = values * values
        for lane in range(0, values.shape[1], 128):
            squares[...] += square[:, lane : lane + 128]
        scaled.append((values * gains[b][...]).astype(BF16))
    for at in range(2):
        for core in range(2):
            total = acc[2 * at + core]
            for b in range(PER):
                total += jnp.dot(scaled[b], weights[b][at][core], preferred_element_type=F32)
            acc[2 * at + core] = total
    total = logits[...]
    for b in range(PER):
        total += lax.dot_general(
            scaled[b], routers[b][...], (((1,), (1,)), ((), ())), preferred_element_type=F32
        )
    logits[...] = total

    if last:

        @pl.when(pl.program_id(0) == pl.num_programs(0) - 1)
        def _():
            mean = jnp.sum(squares[...], axis=1, keepdims=True) / features
            scale = lax.rsqrt(mean + 1e-06)
            gap = jnp.sum(logits[...] * select[...], axis=1, keepdims=True) * scale
            weight[...] = jnp.broadcast_to(1.0 / (1.0 + jnp.exp(-gap)), weight.shape)
            for core in range(2):
                gate = acc[core] * scale
                upper = acc[2 + core] * scale
                width = gate.shape[1]
                hidden[:, core * width : (core + 1) * width] = (
                    gate / (1.0 + jnp.exp(-gate)) * upper
                ).astype(BF16)


def products(rows, places, gate, up, router, gain, carried, select):
    blocks, count, depth = rows.shape
    features, width = gate.shape[1:]
    experts = router.shape[0]
    first, last = carried is None, select is not None
    whole = lambda *shape: pl.BlockSpec(shape, lambda i, order: (0,) * len(shape))

    def weight_spec(b):
        return pl.BlockSpec((2, depth, width), lambda i, order: (0, order[i * PER + b], 0))

    def flat_spec(b, height):
        return pl.BlockSpec((height, depth), lambda i, order: (0, order[i * PER + b]))

    in_specs = [pl.BlockSpec((PER, count, depth), lambda i, order: (i, 0, 0))]
    operands = [rows]
    for b in range(PER):
        in_specs += [weight_spec(b)] * 2
        operands += [gate, up]
    in_specs += [flat_spec(b, experts) for b in range(PER)]
    operands += [router] * PER
    in_specs += [flat_spec(b, 1) for b in range(PER)]
    operands += [gain] * PER
    sums = [(4, count, width), (count, experts), (count, 128)]
    if not first:
        in_specs += [whole(*shape) for shape in sums]
        operands += list(carried)
    scratch = []
    if last:
        in_specs.append(whole(count, experts))
        operands.append(select)
        out_shape = [
            jax.ShapeDtypeStruct((count, 2 * width), BF16),
            jax.ShapeDtypeStruct((count, 128), F32),
        ]
        scratch = [pltpu.VMEM(shape, F32) for shape in sums]
    else:
        out_shape = [jax.ShapeDtypeStruct(shape, F32) for shape in sums]
    return pl.pallas_call(
        lambda *refs: products_kernel(*refs, first=first, last=last, features=features),
        out_shape=out_shape,
        grid_spec=pltpu.PrefetchScalarGridSpec(
            num_scalar_prefetch=1,
            grid=(blocks // PER,),
            in_specs=in_specs,
            out_specs=[whole(*s.shape) for s in out_shape],
            scratch_shapes=scratch,
        ),
        compiler_params=pltpu.CompilerParams(
            dimension_semantics=("arbitrary",), vmem_limit_bytes=VMEM
        ),
        cost_estimate=pl.CostEstimate(
            flops=2 * count * depth * blocks * width * 4,
            bytes_accessed=blocks * depth * width * 8,
            transcendentals=0,
        ),
    )(places, *operands)


def down_kernel(order, hidden, weight, *refs):
    *downs, out = refs
    width = hidden.shape[1] // 2
    for b, ref in enumerate(downs):
        term = jnp.dot(hidden[:, :width], ref[0], preferred_element_type=F32)
        term += jnp.dot(hidden[:, width:], ref[1], preferred_element_type=F32)
        out[b] = (term * weight[:, :1]).astype(BF16)


def down_terms(hidden, weight, places, down, depth):
    count, both = hidden.shape
    blocks = places.shape[0]
    whole = lambda *shape: pl.BlockSpec(shape, lambda i, order: (0,) * len(shape))

    def down_spec(b):
        return pl.BlockSpec(
            (2, both // 2, depth), lambda i, order: (0, 0, order[i * PER + b])
        )

    return pl.pallas_call(
        down_kernel,
        out_shape=jax.ShapeDtypeStruct((blocks, count, depth), BF16),
        grid_spec=pltpu.PrefetchScalarGridSpec(
            num_scalar_prefetch=1,
            grid=(blocks // PER,),
            in_specs=[whole(*hidden.shape), whole(*weight.shape)]
            + [down_spec(b) for b in range(PER)],
            out_specs=pl.BlockSpec((PER, count, depth), lambda i, order: (i, 0, 0)),
        ),
        compiler_params=pltpu.CompilerParams(
            dimension_semantics=("arbitrary",), vmem_limit_bytes=VMEM
        ),
        cost_estimate=pl.CostEstimate(
            flops=2 * count * both * depth * blocks,
            bytes_accessed=both * depth * blocks * 2,
            transcendentals=0,
        ),
    )(places, hidden, weight, *([down] * PER))


def body(
    mixer_out,
    out_proj,
    residual,
    norm_gain,
    router_weight,
    expert_ids,
    expert_gate,
    expert_up,
    expert_down,
):
    node = lax.axis_index("node")
    local = lax.axis_index("local")
    core = lax.axis_index("tp")
    x, y = local // SIDE, local % SIDE
    half_rows, col_width = residual.shape
    capacity = half_rows // 16
    spots = SIDE * capacity
    part = mixer_out.shape[0] // 2

    gate, up, down = (
        lax.all_gather(w, "tp", axis=0, tiled=True) for w in (expert_gate, expert_up, expert_down)
    )

    first, partner = expert_ids[:, 0], expert_ids[:, 1]
    routed = first < SIDE
    relative = lax.rem(first - node + SIDE, SIDE)
    marks = (routed[:, None] & (relative[:, None] == jnp.arange(SIDE)[None, :])).astype(jnp.int32)
    slots = jnp.sum((jnp.cumsum(marks, axis=0) - marks) * marks, axis=1)
    spot = jnp.where(routed, relative * capacity + slots, -1)
    placed = (spot[:, None] == jnp.arange(spots)[None, :]).astype(BF16)
    picked = spot[None, :] == jnp.arange(spots)[:, None]
    partners = jnp.sum(jnp.where(picked, partner[None, :], 0), axis=1).reshape(SIDE, capacity)
    def to_relative(value):
        value = value.reshape((2, SIDE, 2, part) + value.shape[1:])
        value = jnp.where(x % 2 == 1, value[::-1], value)
        return roll_to(value, y, 1)

    spot_rel = to_relative(spot)
    rest_rel = to_relative(residual)
    mine = [((x + p) % SIDE) // 2 == core for p in range(2)]

    groups = []
    for half, (near, far) in enumerate((("x", "y"), ("y", "x"))):
        own = mixer_out[half * part : (half + 1) * part]
        ahead, across, behind = ring(own, near)
        line = jnp.concatenate([own, ahead] + across + [behind], axis=0)
        groups.append([line] + list(ring(line, far)))

    def project(group):
        pieces = group if isinstance(group, list) else [group]
        dots = [jnp.dot(rows, out_proj, preferred_element_type=F32) for rows in pieces]
        return jnp.concatenate(dots, axis=0).reshape(SIDE, part, col_width)

    results = [[project(group) for group in half] for half in groups]

    def split(blocks, p):
        kept = jnp.where(mine[p], blocks[p], blocks[p + 2])
        sent = jnp.where(mine[p], blocks[p + 2], blocks[p])
        return kept, sent

    streams = {}
    for early in (True, False):
        kept, sent, names = [], [], []
        for at in (0, 1, 3) if early else (2,):
            for p in range(2):
                pair = split(results[0][at], p)
                kept.append(pair[0][None])
                sent.append(pair[1][None])
                names.append((0, at, p))
        pair = split(results[1], 1 if early else 0)
        kept.append(pair[0])
        sent.append(pair[1])
        names += [(1, dy, 1 if early else 0) for dy in range(SIDE)]
        kept = jnp.concatenate(kept, axis=0) + swap_core(jnp.concatenate(sent, axis=0))
        for at, (half, dy, p) in enumerate(names):
            streams[half, dy, p] = rest_rel[p, dy, half].astype(F32) + kept[at]

    bucket = jnp.zeros((spots, col_width), F32)
    for late in (False, True):
        names = [n for n in streams if (n[1] == 2 if n[0] == 0 else n[2] == 0) == late]
        where = jnp.concatenate([spot_rel[p, dy, half] for half, dy, p in names])
        one_hot = (where[None, :] == jnp.arange(spots)[:, None]).astype(BF16)
        rows = jnp.concatenate([streams[n] for n in names], axis=0).astype(BF16)
        bucket += jnp.dot(one_hot, rows, preferred_element_type=F32)
    bucket = bucket.astype(BF16).reshape(SIDE, capacity, col_width)

    stream = jnp.stack(
        [streams[half, dy, p] for p in range(2) for dy in range(SIDE) for half in range(2)]
    ).reshape(2, SIDE, 2, part, col_width)
    stream = roll_to(stream, (SIDE - y) % SIDE, 1)
    stream = jnp.where(x % 2 == 1, stream[::-1], stream).reshape(half_rows, col_width)

    tag = jnp.broadcast_to(partners.astype(BF16)[:, :, None], (SIDE, capacity, 128))
    bucket = jnp.concatenate([bucket, tag], axis=2)
    landed = jnp.concatenate(
        [bucket[0]] + [shift_node(bucket[d], d) for d in (1, 3, 2)], axis=0
    )
    partners = landed[:, col_width].astype(jnp.int32)
    landed = landed[:, :col_width]
    experts = jnp.arange(router_weight.shape[1])[None, :]
    select = (experts == node).astype(F32) - (experts == partners[:, None]).astype(F32)
    got = {(-d) % SIDE: shift_mixed(landed, False, d) for d in (1, 3, 2)}
    line = jnp.stack([landed] + [got[d] for d in range(1, SIDE)], axis=0)
    got = {(-d) % SIDE: shift_mixed(line, True, d) for d in (1, 3, 2)}
    arrived = [line] + [got[d] for d in range(1, SIDE)]
    ring_x = ((x + jnp.arange(SIDE)) % SIDE) * SIDE
    ring_y = (y + jnp.arange(SIDE)) % SIDE

    def places(distance):
        return jnp.where(
            core == 0, ring_x + ring_y[distance], ring_x[distance] + ring_y
        ).astype(jnp.int32)

    carried = None
    for d in (0, 1, 3, 2):
        carried = products(
            arrived[d],
            places(d),
            gate,
            up,
            router_weight.T,
            norm_gain[None, :],
            carried,
            select if d == 2 else None,
        )
    hidden, weight = carried

    terms = {d: down_terms(hidden, weight, places(d), down, col_width) for d in (1, 3, 2, 0)}
    got = [shift_mixed(terms[d], True, d) for d in (1, 3, 2)]
    line = sum((g.astype(F32) for g in got), terms[0].astype(F32)).astype(BF16)
    got = [shift_mixed(line[d], False, d) for d in (1, 3, 2)]
    summed = sum((g.astype(F32) for g in got), line[0].astype(F32)).astype(BF16)
    summed = summed.reshape(SIDE, capacity, col_width)
    back = {d: shift_node(summed[at], -d) for at, d in ((1, 1), (2, 3), (3, 2))}
    returned = jnp.concatenate([summed[0]] + [back[d] for d in range(1, SIDE)], axis=0)
    expert_sum = jnp.dot(placed, returned, preferred_element_type=F32)
    return (stream + expert_sum).astype(BF16)


def solution(mesh):
    placed = (
        P(("node", "local"), "tp"),
        P("tp", "local"),
        P(("node", "tp"), "local"),
        P(),
        P(),
        P(("node", "tp"), None),
        P("node", None, ("local", "tp")),
        P("node", None, ("local", "tp")),
        P("node", ("local", "tp"), None),
    )
    return jax.shard_map(
        body, mesh=mesh, in_specs=placed, out_specs=P(("node", "tp"), "local"), check_vma=False
    )
```

```python
import functools

import jax
import jax.numpy as jnp
from jax import lax
from jax.experimental import pallas as pl
from jax.experimental.pallas import tpu as pltpu
from jax.sharding import PartitionSpec as P

SIDE = 4
PER = 1
VMEM = 8 * 1024 * 1024
F32 = jnp.float32
BF16 = jnp.bfloat16


def shift_node(value, by):
    return lax.ppermute(value, "node", [(i, (i + by) % SIDE) for i in range(SIDE)])


def shift(value, axis, by):
    dx, dy = (by, 0) if axis == "x" else (0, by)
    pairs = [
        (x * SIDE + y, ((x + dx) % SIDE) * SIDE + (y + dy) % SIDE)
        for x in range(SIDE)
        for y in range(SIDE)
    ]
    return lax.ppermute(value, "local", pairs)


def shift_mixed(value, far, by):
    pairs = []
    for x in range(SIDE):
        for y in range(SIDE):
            for core in range(2):
                dx, dy = (by, 0) if (core == 0) != far else (0, by)
                to = ((x + dx) % SIDE) * SIDE + (y + dy) % SIDE
                pairs.append(((x * SIDE + y) * 2 + core, to * 2 + core))
    return lax.ppermute(value, ("local", "tp"), pairs)


def swap_core(value):
    return lax.ppermute(value, "tp", [(0, 1), (1, 0)])


def roll_to(value, by, axis):
    doubled = jnp.concatenate([value, value], axis=axis)
    return lax.dynamic_slice_in_dim(doubled, by, value.shape[axis], axis)


def ring(value, axis):
    half = value.shape[0] // 2
    behind = shift(value, axis, 1)
    ahead = shift(value, axis, -1)
    across = [shift(behind[:half], axis, 1), shift(ahead[half:], axis, -1)]
    return ahead, across, behind


def first_kernel(order, rows, early, *refs, first, last, features):
    weights, refs = [refs[2 * b : 2 * b + 2] for b in range(PER)], refs[2 * PER :]
    routers, refs = refs[:PER], refs[PER:]
    gains, refs = refs[:PER], refs[PER:]
    carried = None
    if not first:
        carried, refs = refs[:3], refs[3:]
    if last:
        select, hidden, weight, acc, logits, squares = refs
    else:
        acc, logits, squares = refs

    @pl.when(pl.program_id(0) == 0)
    def _():
        for at, ref in enumerate((acc, logits, squares)):
            ref[...] = jnp.zeros_like(ref) if first else carried[at][...]

    scaled = []
    for b in range(PER):
        values = rows[b].astype(F32)
        square = values * values
        for lane in range(0, values.shape[1], 128):
            squares[...] += square[:, lane : lane + 128]
        scaled.append((values * gains[b][...]).astype(BF16))
    for at in range(2):
        for core in range(2):
            total = acc[2 * at + core]
            for b in range(PER):
                total += jnp.dot(scaled[b], weights[b][at][core], preferred_element_type=F32)
            acc[2 * at + core] = total
    total = logits[...]
    for b in range(PER):
        total += lax.dot_general(
            scaled[b], routers[b][...], (((1,), (1,)), ((), ())), preferred_element_type=F32
        )
    logits[...] = total

    if last:

        @pl.when(pl.program_id(0) == pl.num_programs(0) - 1)
        def _():
            mean = jnp.sum(squares[...], axis=1, keepdims=True) / features
            scale = lax.rsqrt(mean + 1e-06)
            gap = jnp.sum(logits[...] * select[...], axis=1, keepdims=True) * scale
            weight[...] = jnp.broadcast_to(1.0 / (1.0 + jnp.exp(-gap)), weight.shape)
            for core in range(2):
                gate = acc[core] * scale
                upper = acc[2 + core] * scale
                width = gate.shape[1]
                hidden[:, core * width : (core + 1) * width] = (
                    gate / (1.0 + jnp.exp(-gate)) * upper
                ).astype(BF16)


def first_products(rows, places, gate, up, router, gain, carried, select, early):
    blocks, count, depth = rows.shape
    features, width = gate.shape[1:]
    experts = router.shape[0]
    first, last = carried is None, select is not None
    whole = lambda *shape: pl.BlockSpec(shape, lambda i, order: (0,) * len(shape))

    def weight_spec(b):
        return pl.BlockSpec((2, depth, width), lambda i, order: (0, order[i * PER + b], 0))

    def flat_spec(b, height):
        return pl.BlockSpec((height, depth), lambda i, order: (0, order[i * PER + b]))

    in_specs = [
        pl.BlockSpec((PER, count, depth), lambda i, order: (i, 0, 0)),
        pl.BlockSpec((1, 8, 128), lambda i, order: (0, 0, 0)),
    ]
    operands = [rows, in_hbm(early)]
    for b in range(PER):
        in_specs += [weight_spec(b)] * 2
        operands += [in_hbm(gate), in_hbm(up)]
    in_specs += [flat_spec(b, experts) for b in range(PER)]
    operands += [router] * PER
    in_specs += [flat_spec(b, 1) for b in range(PER)]
    operands += [gain] * PER
    sums = [(4, count, width), (count, experts), (count, 128)]
    if not first:
        in_specs += [whole(*shape) for shape in sums]
        operands += list(carried)
    scratch = []
    if last:
        in_specs.append(whole(count, experts))
        operands.append(select)
        out_shape = [
            jax.ShapeDtypeStruct((count, 2 * width), BF16),
            jax.ShapeDtypeStruct((count, 128), F32),
        ]
        scratch = [pltpu.VMEM(shape, F32) for shape in sums]
    else:
        out_shape = [jax.ShapeDtypeStruct(shape, F32) for shape in sums]
    return pl.pallas_call(
        lambda *refs: first_kernel(*refs, first=first, last=last, features=features),
        out_shape=out_shape,
        grid_spec=pltpu.PrefetchScalarGridSpec(
            num_scalar_prefetch=1,
            grid=(blocks // PER,),
            in_specs=in_specs,
            out_specs=[whole(*s.shape) for s in out_shape],
            scratch_shapes=scratch,
        ),
        compiler_params=pltpu.CompilerParams(
            dimension_semantics=("arbitrary",), vmem_limit_bytes=VMEM
        ),
        cost_estimate=pl.CostEstimate(
            flops=2 * count * depth * blocks * width * 4,
            bytes_accessed=blocks * depth * width * 8,
            transcendentals=0,
        ),
    )(places, *operands)


def in_hbm(value):
    return pltpu.with_memory_space_constraint(value, pltpu.HBM)


def in_vmem(value):
    return pltpu.with_memory_space_constraint(value, pltpu.VMEM)


def products_kernel(order, rows, gate, up, router, gain, *refs, first, last, features):
    carried = None
    if not first:
        carried, refs = refs[:3], refs[3:]
    if last:
        select, hidden, weight = refs
    else:
        acc, logits, squares = refs
    count, depth, width = rows.shape[1], rows.shape[2], gate.shape[2]
    scaled, spans = [], []
    square_sum = jnp.zeros((count, 128), F32) if first else carried[2][...]
    for b in range(SIDE):
        span = pl.ds(pl.multiple_of(order[b] * depth, depth), depth)
        values = rows[b].astype(F32)
        square = values * values
        for lane in range(0, depth, 128):
            square_sum += square[:, lane : lane + 128]
        scaled.append((values * gain[:, span]).astype(BF16))
        spans.append(span)
    totals = []
    for at, matrix in enumerate((gate, up)):
        for core in range(2):
            total = jnp.zeros((count, width), F32) if first else carried[0][2 * at + core]
            for values, span in zip(scaled, spans):
                total += jnp.dot(values, matrix[core, span, :], preferred_element_type=F32)
            if last:
                totals.append(total)
            else:
                acc[2 * at + core] = total
    total = jnp.zeros((count, router.shape[0]), F32) if first else carried[1][...]
    for values, span in zip(scaled, spans):
        total += lax.dot_general(
            values, router[:, span], (((1,), (1,)), ((), ())), preferred_element_type=F32
        )
    if not last:
        logits[...] = total
        squares[...] = square_sum
        return
    mean = jnp.sum(square_sum, axis=1, keepdims=True) / features
    scale = lax.rsqrt(mean + 1e-06)
    gap = jnp.sum(total * select[...], axis=1, keepdims=True) * scale
    weight[...] = jnp.broadcast_to(1.0 / (1.0 + jnp.exp(-gap)), weight.shape)
    for core in range(2):
        gated = totals[core] * scale
        upper = totals[2 + core] * scale
        hidden[:, core * width : (core + 1) * width] = (
            gated / (1.0 + jnp.exp(-gated)) * upper
        ).astype(BF16)


def local_call(kernel, places, operands, out_shape, flops, touched):
    smem, vmem = (pl.BlockSpec(memory_space=m) for m in (pltpu.SMEM, pltpu.VMEM))
    return pl.pallas_call(
        kernel,
        out_shape=out_shape,
        in_specs=[smem] + [vmem] * len(operands),
        out_specs=jax.tree.map(lambda _: vmem, out_shape),
        compiler_params=pltpu.CompilerParams(vmem_limit_bytes=VMEM),
        cost_estimate=pl.CostEstimate(flops=flops, bytes_accessed=touched, transcendentals=0),
    )(places, *operands)


def products(rows, places, gate, up, router, gain, carried, select):
    blocks, count, depth = rows.shape
    features, width = gate.shape[1:]
    first, last = carried is None, select is not None
    operands = [rows, in_vmem(gate), in_vmem(up), router, gain]
    operands += [] if first else list(carried)
    if last:
        operands.append(select)
        out_shape = [
            jax.ShapeDtypeStruct((count, 2 * width), BF16),
            jax.ShapeDtypeStruct((count, 128), F32),
        ]
    else:
        sums = [(4, count, width), (count, router.shape[0]), (count, 128)]
        out_shape = [jax.ShapeDtypeStruct(shape, F32) for shape in sums]
    return local_call(
        lambda *refs: products_kernel(*refs, first=first, last=last, features=features),
        places,
        operands,
        out_shape,
        2 * count * depth * blocks * width * 4,
        blocks * depth * width * 8,
    )


def down_kernel(order, hidden, weight, down, out):
    width, depth = hidden.shape[1] // 2, out.shape[2]
    for b in range(SIDE):
        span = pl.ds(pl.multiple_of(order[b] * depth, depth), depth)
        term = jnp.dot(hidden[:, :width], down[0, :, span], preferred_element_type=F32)
        term += jnp.dot(hidden[:, width:], down[1, :, span], preferred_element_type=F32)
        out[b] = (term * weight[:, :1]).astype(BF16)


def down_terms(hidden, weight, places, down, depth):
    count, both = hidden.shape
    return local_call(
        down_kernel,
        places,
        [hidden, weight, in_vmem(down)],
        jax.ShapeDtypeStruct((SIDE, count, depth), BF16),
        2 * count * both * depth * SIDE,
        both * depth * SIDE * 2,
    )


def body(
    mixer_out,
    out_proj,
    residual,
    norm_gain,
    router_weight,
    expert_ids,
    expert_gate,
    expert_up,
    expert_down,
):
    node = lax.axis_index("node")
    local = lax.axis_index("local")
    core = lax.axis_index("tp")
    x, y = local // SIDE, local % SIDE
    half_rows, col_width = residual.shape
    capacity = half_rows // 16
    spots = SIDE * capacity
    part = mixer_out.shape[0] // 2

    gate, up, down = (
        lax.all_gather(w, "tp", axis=0, tiled=True) for w in (expert_gate, expert_up, expert_down)
    )

    first, partner = expert_ids[:, 0], expert_ids[:, 1]
    routed = first < SIDE
    relative = lax.rem(first - node + SIDE, SIDE)
    marks = (routed[:, None] & (relative[:, None] == jnp.arange(SIDE)[None, :])).astype(jnp.int32)
    slots = jnp.sum((jnp.cumsum(marks, axis=0) - marks) * marks, axis=1)
    spot = jnp.where(routed, relative * capacity + slots, -1)
    placed = (spot[:, None] == jnp.arange(spots)[None, :]).astype(BF16)
    picked = spot[None, :] == jnp.arange(spots)[:, None]
    partners = jnp.sum(jnp.where(picked, partner[None, :], 0), axis=1).reshape(SIDE, capacity)
    def to_relative(value):
        value = value.reshape((2, SIDE, 2, part) + value.shape[1:])
        value = jnp.where(x % 2 == 1, value[::-1], value)
        return roll_to(value, y, 1)

    spot_rel = to_relative(spot)
    rest_rel = to_relative(residual)
    mine = [((x + p) % SIDE) // 2 == core for p in range(2)]

    groups = []
    for half, (near, far) in enumerate((("x", "y"), ("y", "x"))):
        own = mixer_out[half * part : (half + 1) * part]
        ahead, across, behind = ring(own, near)
        line = jnp.concatenate([own, ahead] + across + [behind], axis=0)
        groups.append([line] + list(ring(line, far)))

    def project(group):
        pieces = group if isinstance(group, list) else [group]
        dots = [jnp.dot(rows, out_proj, preferred_element_type=F32) for rows in pieces]
        return jnp.concatenate(dots, axis=0).reshape(SIDE, part, col_width)

    results = [[project(group) for group in half] for half in groups]

    def split(blocks, p):
        kept = jnp.where(mine[p], blocks[p], blocks[p + 2])
        sent = jnp.where(mine[p], blocks[p + 2], blocks[p])
        return kept, sent

    streams = {}
    for early in (True, False):
        kept, sent, names = [], [], []
        for at in (0, 1, 3) if early else (2,):
            for p in range(2):
                pair = split(results[0][at], p)
                kept.append(pair[0][None])
                sent.append(pair[1][None])
                names.append((0, at, p))
        pair = split(results[1], 1 if early else 0)
        kept.append(pair[0])
        sent.append(pair[1])
        names += [(1, dy, 1 if early else 0) for dy in range(SIDE)]
        kept = jnp.concatenate(kept, axis=0) + swap_core(jnp.concatenate(sent, axis=0))
        for at, (half, dy, p) in enumerate(names):
            streams[half, dy, p] = rest_rel[p, dy, half].astype(F32) + kept[at]

    bucket = jnp.zeros((spots, col_width), F32)
    for late in (False, True):
        names = [n for n in streams if (n[1] == 2 if n[0] == 0 else n[2] == 0) == late]
        where = jnp.concatenate([spot_rel[p, dy, half] for half, dy, p in names])
        one_hot = (where[None, :] == jnp.arange(spots)[:, None]).astype(BF16)
        rows = jnp.concatenate([streams[n] for n in names], axis=0).astype(BF16)
        bucket += jnp.dot(one_hot, rows, preferred_element_type=F32)
    bucket = bucket.astype(BF16).reshape(SIDE, capacity, col_width)

    stream = jnp.stack(
        [streams[half, dy, p] for p in range(2) for dy in range(SIDE) for half in range(2)]
    ).reshape(2, SIDE, 2, part, col_width)
    stream = roll_to(stream, (SIDE - y) % SIDE, 1)
    stream = jnp.where(x % 2 == 1, stream[::-1], stream).reshape(half_rows, col_width)

    tag = jnp.broadcast_to(partners.astype(BF16)[:, :, None], (SIDE, capacity, 128))
    bucket = jnp.concatenate([bucket, tag], axis=2)
    landed = jnp.concatenate(
        [bucket[0]] + [shift_node(bucket[d], d) for d in (1, 3, 2)], axis=0
    )
    partners = landed[:, col_width].astype(jnp.int32)
    landed = landed[:, :col_width]
    experts = jnp.arange(router_weight.shape[1])[None, :]
    select = (experts == node).astype(F32) - (experts == partners[:, None]).astype(F32)
    got = {(-d) % SIDE: shift_mixed(landed, False, d) for d in (1, 3, 2)}
    line = jnp.stack([landed] + [got[d] for d in range(1, SIDE)], axis=0)
    got = {(-d) % SIDE: shift_mixed(line, True, d) for d in (1, 3, 2)}
    arrived = [line] + [got[d] for d in range(1, SIDE)]
    ring_x = ((x + jnp.arange(SIDE)) % SIDE) * SIDE
    ring_y = (y + jnp.arange(SIDE)) % SIDE

    def places(distance):
        return jnp.where(
            core == 0, ring_x + ring_y[distance], ring_x[distance] + ring_y
        ).astype(jnp.int32)

    carried = None
    for d in (0, 1, 3, 2):
        carried = (functools.partial(first_products, early=down) if d == 0 else products)(
            arrived[d],
            places(d),
            gate,
            up,
            router_weight.T,
            norm_gain[None, :],
            carried,
            select if d == 2 else None,
        )
    hidden, weight = carried

    terms = {d: down_terms(hidden, weight, places(d), down, col_width) for d in (1, 3, 2, 0)}
    got = [shift_mixed(terms[d], True, d) for d in (1, 3, 2)]
    line = sum((g.astype(F32) for g in got), terms[0].astype(F32)).astype(BF16)
    got = [shift_mixed(line[d], False, d) for d in (1, 3, 2)]
    summed = sum((g.astype(F32) for g in got), line[0].astype(F32)).astype(BF16)
    summed = summed.reshape(SIDE, capacity, col_width)
    back = {d: shift_node(summed[at], -d) for at, d in ((1, 1), (2, 3), (3, 2))}
    returned = jnp.concatenate([summed[0]] + [back[d] for d in range(1, SIDE)], axis=0)
    expert_sum = jnp.dot(placed, returned, preferred_element_type=F32)
    return (stream + expert_sum).astype(BF16)


def solution(mesh):
    placed = (
        P(("node", "local"), "tp"),
        P("tp", "local"),
        P(("node", "tp"), "local"),
        P(),
        P(),
        P(("node", "tp"), None),
        P("node", None, ("local", "tp")),
        P("node", None, ("local", "tp")),
        P("node", ("local", "tp"), None),
    )
    return jax.shard_map(
        body, mesh=mesh, in_specs=placed, out_specs=P(("node", "tp"), "local"), check_vma=False
    )
```

```python
import functools

import jax
import jax.numpy as jnp
from jax import lax
from jax.experimental import pallas as pl
from jax.experimental.pallas import tpu as pltpu
from jax.sharding import PartitionSpec as P

SIDE = 4
PER = 1
VMEM = 8 * 1024 * 1024
F32 = jnp.float32
BF16 = jnp.bfloat16


def shift_node(value, by):
    return lax.ppermute(value, "node", [(i, (i + by) % SIDE) for i in range(SIDE)])


def shift_mixed(value, far, by):
    pairs = []
    for x in range(SIDE):
        for y in range(SIDE):
            for core in range(2):
                dx, dy = (by, 0) if (core == 0) != far else (0, by)
                to = ((x + dx) % SIDE) * SIDE + (y + dy) % SIDE
                pairs.append(((x * SIDE + y) * 2 + core, to * 2 + core))
    return lax.ppermute(value, ("local", "tp"), pairs)


def swap_core(value):
    return lax.ppermute(value, "tp", [(0, 1), (1, 0)])


EARLY_0 = [(p, dy) for dy in (1, 3) for p in range(2)]
EARLY_1 = [(1, dy) for dy in range(SIDE)]
LATE_0 = [(p, dy) for dy in (0, 2) for p in range(2)]
LATE_1 = [(0, dy) for dy in range(SIDE)]


def combine_kernel(flags, *refs):
    lows, highs, refs = refs[:SIDE], refs[SIDE : 2 * SIDE], refs[2 * SIDE :]
    early, late, residual, one_hot, tag, stream, *outs, rows = refs
    part, width = residual.shape[1:]
    first = flags[0] == 1

    def block(far, near):
        half = (lows if near < 2 else highs)[far]
        return half[near % 2 * part : (near % 2 + 1) * part, :]

    for p in range(2):
        mine = flags[1 + p] == 1
        for dy in range(SIDE):
            along_x = jnp.where(mine, block(dy, p), block(dy, p + 2))
            along_y = jnp.where(mine, block(p, dy), block(p + 2, dy))
            kept = jnp.where(first, along_x, along_y)
            at_0 = early[EARLY_1.index((p, dy))] if p == 1 else late[LATE_1.index((p, dy))]
            if dy in (1, 3):
                at_1 = early[EARLY_0.index((p, dy))]
            else:
                at_1 = late[LATE_0.index((p, dy))]
            got = jnp.where(first, at_0.astype(F32), at_1.astype(F32))
            at = flags[3 + p] * SIDE + flags[5 + dy]
            value = residual[at].astype(F32) + (kept + got)
            stream[at] = value
            rows[pl.ds(pl.multiple_of(at * part, part), part), :] = value.astype(BF16)
    picked = jnp.dot(one_hot[...], rows[...], preferred_element_type=F32).astype(BF16)
    for d, out in enumerate(outs):
        count = out.shape[0] - tag.shape[1]
        out[:count, :] = picked[d * count : (d + 1) * count]
        out[count:, :] = tag[d]


def combine(flags, lows, highs, early, late, residual, one_hot, tag):
    part, width = residual.shape[1:]
    spots = one_hot.shape[0]
    operands = [in_hbm(v) for v in (*lows, *highs, early, late, residual)] + [one_hot, tag]
    out_shape = [jax.ShapeDtypeStruct((2 * SIDE, part, width), F32)]
    out_shape += [jax.ShapeDtypeStruct((spots // SIDE + tag.shape[1], width), BF16)] * SIDE
    smem, vmem = (pl.BlockSpec(memory_space=m) for m in (pltpu.SMEM, pltpu.VMEM))
    return pl.pallas_call(
        combine_kernel,
        out_shape=out_shape,
        in_specs=[smem] + [vmem] * len(operands),
        out_specs=[vmem] * len(out_shape),
        scratch_shapes=[pltpu.VMEM((2 * SIDE * part, width), BF16)],
        compiler_params=pltpu.CompilerParams(vmem_limit_bytes=16 * 1024 * 1024),
        cost_estimate=pl.CostEstimate(
            flops=2 * spots * 2 * SIDE * part * width, bytes_accessed=1 << 22, transcendentals=0
        ),
    )(flags, *operands)


def halves(one, other, early):
    def kernel(one, other, early, first, second, sems):
        half = first.shape[0]
        copies = [
            pltpu.make_async_copy(one.at[pl.ds(0, half)], first, sems.at[0]),
            pltpu.make_async_copy(other.at[pl.ds(half, half)], second, sems.at[1]),
        ]
        for copy in copies:
            copy.start()
        for copy in copies:
            copy.wait()

    shape = jax.ShapeDtypeStruct((one.shape[0] // 2,) + one.shape[1:], one.dtype)
    anywhere = pl.BlockSpec(memory_space=pl.ANY)
    return pl.pallas_call(
        kernel,
        out_shape=[shape, shape],
        in_specs=[anywhere] * 3,
        out_specs=[anywhere] * 2,
        scratch_shapes=[pltpu.SemaphoreType.DMA((2,))],
        compiler_params=pltpu.CompilerParams(vmem_limit_bytes=1024 * 1024),
        cost_estimate=pl.CostEstimate(
            flops=0, bytes_accessed=2 * one.size * 2, transcendentals=0
        ),
    )(one, other, early)


def first_kernel(order, rows, early, *refs, first, last, features):
    weights, refs = [refs[2 * b : 2 * b + 2] for b in range(PER)], refs[2 * PER :]
    routers, refs = refs[:PER], refs[PER:]
    gains, refs = refs[:PER], refs[PER:]
    carried = None
    if not first:
        carried, refs = refs[:3], refs[3:]
    if last:
        select, hidden, weight, acc, logits, squares = refs
    else:
        acc, logits, squares = refs

    @pl.when(pl.program_id(0) == 0)
    def _():
        for at, ref in enumerate((acc, logits, squares)):
            ref[...] = jnp.zeros_like(ref) if first else carried[at][...]

    scaled = []
    for b in range(PER):
        values = rows[b].astype(F32)
        square = values * values
        for lane in range(0, values.shape[1], 128):
            squares[...] += square[:, lane : lane + 128]
        scaled.append((values * gains[b][...]).astype(BF16))
    for at in range(2):
        for core in range(2):
            total = acc[2 * at + core]
            for b in range(PER):
                total += jnp.dot(scaled[b], weights[b][at][core], preferred_element_type=F32)
            acc[2 * at + core] = total
    total = logits[...]
    for b in range(PER):
        total += lax.dot_general(
            scaled[b], routers[b][...], (((1,), (1,)), ((), ())), preferred_element_type=F32
        )
    logits[...] = total

    if last:

        @pl.when(pl.program_id(0) == pl.num_programs(0) - 1)
        def _():
            mean = jnp.sum(squares[...], axis=1, keepdims=True) / features
            scale = lax.rsqrt(mean + 1e-06)
            gap = jnp.sum(logits[...] * select[...], axis=1, keepdims=True) * scale
            weight[...] = jnp.broadcast_to(1.0 / (1.0 + jnp.exp(-gap)), weight.shape)
            for core in range(2):
                gate = acc[core] * scale
                upper = acc[2 + core] * scale
                width = gate.shape[1]
                hidden[:, core * width : (core + 1) * width] = (
                    gate / (1.0 + jnp.exp(-gate)) * upper
                ).astype(BF16)


def first_products(rows, places, gate, up, router, gain, carried, select, early):
    blocks, count, depth = rows.shape
    features, width = gate.shape[1:]
    experts = router.shape[0]
    first, last = carried is None, select is not None
    whole = lambda *shape: pl.BlockSpec(shape, lambda i, order: (0,) * len(shape))

    def weight_spec(b):
        return pl.BlockSpec((2, depth, width), lambda i, order: (0, order[i * PER + b], 0))

    def flat_spec(b, height):
        return pl.BlockSpec((height, depth), lambda i, order: (0, order[i * PER + b]))

    in_specs = [
        pl.BlockSpec((PER, count, depth), lambda i, order: (i, 0, 0)),
        pl.BlockSpec((1, 8, 128), lambda i, order: (0, 0, 0)),
    ]
    operands = [rows, in_hbm(early)]
    for b in range(PER):
        in_specs += [weight_spec(b)] * 2
        operands += [in_hbm(gate), in_hbm(up)]
    in_specs += [flat_spec(b, experts) for b in range(PER)]
    operands += [router] * PER
    in_specs += [flat_spec(b, 1) for b in range(PER)]
    operands += [gain] * PER
    sums = [(4, count, width), (count, experts), (count, 128)]
    if not first:
        in_specs += [whole(*shape) for shape in sums]
        operands += list(carried)
    scratch = []
    if last:
        in_specs.append(whole(count, experts))
        operands.append(select)
        out_shape = [
            jax.ShapeDtypeStruct((count, 2 * width), BF16),
            jax.ShapeDtypeStruct((count, 128), F32),
        ]
        scratch = [pltpu.VMEM(shape, F32) for shape in sums]
    else:
        out_shape = [jax.ShapeDtypeStruct(shape, F32) for shape in sums]
    return pl.pallas_call(
        lambda *refs: first_kernel(*refs, first=first, last=last, features=features),
        out_shape=out_shape,
        grid_spec=pltpu.PrefetchScalarGridSpec(
            num_scalar_prefetch=1,
            grid=(blocks // PER,),
            in_specs=in_specs,
            out_specs=[whole(*s.shape) for s in out_shape],
            scratch_shapes=scratch,
        ),
        compiler_params=pltpu.CompilerParams(
            dimension_semantics=("arbitrary",), vmem_limit_bytes=VMEM
        ),
        cost_estimate=pl.CostEstimate(
            flops=2 * count * depth * blocks * width * 4,
            bytes_accessed=blocks * depth * width * 8,
            transcendentals=0,
        ),
    )(places, *operands)


def in_hbm(value):
    return pltpu.with_memory_space_constraint(value, pltpu.HBM)


def in_vmem(value):
    return pltpu.with_memory_space_constraint(value, pltpu.VMEM)


def products_kernel(order, *refs, pieces, distances, last, features):
    rows, refs = refs[:pieces], refs[pieces:]
    gate, up, router, gain, *refs = refs
    carried, refs = refs[:3], refs[3:]
    if last:
        select, hidden, weight = refs
    else:
        acc, logits, squares = refs
    count, depth = rows[0].shape[1:]
    width = gate.shape[2]
    scaled, spans = [], []
    square_sum = carried[2][...]
    arrived = [(ref, at) for ref in rows for at in range(ref.shape[0])]
    for b, (ref, at) in enumerate(arrived):
        block = order[distances[b // SIDE] * SIDE + b % SIDE]
        span = pl.ds(pl.multiple_of(block * depth, depth), depth)
        values = ref[at].astype(F32)
        square = values * values
        for lane in range(0, depth, 128):
            square_sum += square[:, lane : lane + 128]
        scaled.append((values * gain[:, span]).astype(BF16))
        spans.append(span)
    totals = []
    for at, matrix in enumerate((gate, up)):
        for core in range(2):
            total = carried[0][2 * at + core]
            for values, span in zip(scaled, spans):
                total += jnp.dot(values, matrix[core, span, :], preferred_element_type=F32)
            if last:
                totals.append(total)
            else:
                acc[2 * at + core] = total
    total = carried[1][...]
    for values, span in zip(scaled, spans):
        total += lax.dot_general(
            values, router[:, span], (((1,), (1,)), ((), ())), preferred_element_type=F32
        )
    if not last:
        logits[...] = total
        squares[...] = square_sum
        return
    mean = jnp.sum(square_sum, axis=1, keepdims=True) / features
    scale = lax.rsqrt(mean + 1e-06)
    gap = jnp.sum(total * select[...], axis=1, keepdims=True) * scale
    weight[...] = jnp.broadcast_to(1.0 / (1.0 + jnp.exp(-gap)), weight.shape)
    for core in range(2):
        gated = totals[core] * scale
        upper = totals[2 + core] * scale
        hidden[:, core * width : (core + 1) * width] = (
            gated / (1.0 + jnp.exp(-gated)) * upper
        ).astype(BF16)


def local_call(kernel, places, operands, out_shape, flops, touched):
    smem, vmem = (pl.BlockSpec(memory_space=m) for m in (pltpu.SMEM, pltpu.VMEM))
    return pl.pallas_call(
        kernel,
        out_shape=out_shape,
        in_specs=[smem] + [vmem] * len(operands),
        out_specs=jax.tree.map(lambda _: vmem, out_shape),
        compiler_params=pltpu.CompilerParams(vmem_limit_bytes=VMEM),
        cost_estimate=pl.CostEstimate(flops=flops, bytes_accessed=touched, transcendentals=0),
    )(places, *operands)


def products(rows, places, distances, gate, up, router, gain, carried, select):
    count, depth = rows[0].shape[1:]
    blocks = SIDE * len(distances)
    features, width = gate.shape[1:]
    last = select is not None
    operands = [*rows, in_vmem(gate), in_vmem(up), router, gain, *map(in_vmem, carried)]
    if last:
        operands.append(select)
        out_shape = [
            jax.ShapeDtypeStruct((count, 2 * width), BF16),
            jax.ShapeDtypeStruct((count, 128), F32),
        ]
    else:
        sums = [(4, count, width), (count, router.shape[0]), (count, 128)]
        out_shape = [jax.ShapeDtypeStruct(shape, F32) for shape in sums]
    return local_call(
        lambda *refs: products_kernel(
            *refs, pieces=len(rows), distances=distances, last=last, features=features
        ),
        places,
        operands,
        out_shape,
        2 * count * depth * blocks * width * 4,
        blocks * depth * width * 8,
    )


def down_kernel(order, hidden, weight, down, *outs, distance):
    width, depth = hidden.shape[1] // 2, outs[0].shape[2]
    for b in range(SIDE):
        span = pl.ds(pl.multiple_of(order[distance * SIDE + b] * depth, depth), depth)
        term = jnp.dot(hidden[:, :width], down[0, :, span], preferred_element_type=F32)
        term += jnp.dot(hidden[:, width:], down[1, :, span], preferred_element_type=F32)
        term = (term * weight[:, :1]).astype(BF16)
        for at, out in enumerate(outs):
            out[b] = term[at * out.shape[1] : (at + 1) * out.shape[1]]


def down_terms(hidden, weight, places, distance, down, depth, parts):
    count, both = hidden.shape
    return local_call(
        functools.partial(down_kernel, distance=distance),
        places,
        [hidden, weight, in_vmem(down)],
        [jax.ShapeDtypeStruct((SIDE, count // parts, depth), BF16)] * parts,
        2 * count * both * depth * SIDE,
        both * depth * SIDE * 2,
    )


def body(
    mixer_out,
    out_proj,
    residual,
    norm_gain,
    router_weight,
    expert_ids,
    expert_gate,
    expert_up,
    expert_down,
):
    node = lax.axis_index("node")
    local = lax.axis_index("local")
    core = lax.axis_index("tp")
    x, y = local // SIDE, local % SIDE
    half_rows, col_width = residual.shape
    capacity = half_rows // 16
    spots = SIDE * capacity
    part = mixer_out.shape[0]

    gate, up, down = (
        lax.all_gather(w, "tp", axis=0, tiled=True) for w in (expert_gate, expert_up, expert_down)
    )

    first, partner = expert_ids[:, 0], expert_ids[:, 1]
    routed = first < SIDE
    relative = lax.rem(first - node + SIDE, SIDE)
    marks = (routed[:, None] & (relative[:, None] == jnp.arange(SIDE)[None, :])).astype(jnp.int32)
    slots = jnp.sum((jnp.cumsum(marks, axis=0) - marks) * marks, axis=1)
    spot = jnp.where(routed, relative * capacity + slots, -1)
    placed = (spot[:, None] == jnp.arange(spots)[None, :]).astype(BF16)
    picked = spot[None, :] == jnp.arange(spots)[:, None]
    partners = jnp.sum(jnp.where(picked, partner[None, :], 0), axis=1).reshape(SIDE, capacity)
    mine = [((x + p) % SIDE) // 2 == core for p in range(2)]

    ahead, behind = shift_mixed(mixer_out, False, -1), shift_mixed(mixer_out, False, 1)
    across = [
        shift_mixed(behind[: part // 2], False, 1),
        shift_mixed(ahead[part // 2 :], False, -1),
    ]
    low = jnp.concatenate([mixer_out, ahead], axis=0)
    low_1, low_3 = shift_mixed(low, True, -1), shift_mixed(low, True, 1)
    high = jnp.concatenate(across + [behind], axis=0)
    high_1, high_3 = shift_mixed(high, True, -1), shift_mixed(high, True, 1)
    low_2, high_2 = shift_mixed(low_3, True, 1), shift_mixed(high_1, True, -1)

    def project(rows):
        return lax.optimization_barrier(jnp.dot(rows, out_proj, preferred_element_type=F32))

    lows = [project(rows) for rows in (low, low_1, low_2, low_3)]
    highs = [project(rows) for rows in (high, high_1, high_2, high_3)]

    def block(far, near):
        half = (lows if near < 2 else highs)[far]
        return half[near % 2 * part : (near % 2 + 1) * part]

    def sent(names_0, names_1):
        out = []
        for (p, dy), (q, ey) in zip(names_0, names_1):
            along_x = jnp.where(mine[p], block(dy, p + 2), block(dy, p))
            along_y = jnp.where(mine[q], block(q + 2, ey), block(q, ey))
            out.append(jnp.where(core == 0, along_x, along_y))
        return jnp.stack(out).astype(BF16)

    got_early, got_late = swap_core(sent(EARLY_0, EARLY_1)), swap_core(sent(LATE_0, LATE_1))
    tag = jnp.zeros((SIDE, 16, col_width), BF16).at[:, 0, :capacity].set(partners.astype(BF16))
    flags = [core == 0] + mine + [(x + p) % 2 for p in range(2)] + [(y + dy) % SIDE for dy in range(SIDE)]
    stream, *bucket = combine(
        jnp.stack([f.astype(jnp.int32) for f in flags]),
        lows,
        highs,
        got_early,
        got_late,
        residual.reshape(2 * SIDE, part, col_width),
        picked.astype(BF16),
        tag,
    )
    stream = stream.reshape(half_rows, col_width)

    landed = [bucket[0]] + [shift_node(bucket[d], d) for d in (1, 3, 2)]
    partners = jnp.concatenate([v[capacity, :capacity] for v in landed]).astype(jnp.int32)
    landed = jnp.concatenate([v[:capacity] for v in landed], axis=0)
    experts = jnp.arange(router_weight.shape[1])[None, :]
    select = (experts == node).astype(F32) - (experts == partners[:, None]).astype(F32)
    got = {(-d) % SIDE: shift_mixed(landed, False, d) for d in (1, 3, 2)}
    line = jnp.stack([landed] + [got[d] for d in range(1, SIDE)], axis=0)
    ahead, behind = shift_mixed(line, True, -1), shift_mixed(line, True, 1)
    ring_x = ((x + jnp.arange(SIDE)) % SIDE) * SIDE
    ring_y = (y + jnp.arange(SIDE)) % SIDE
    order = jnp.where(
        core == 0, ring_x[None, :] + ring_y[:, None], ring_x[:, None] + ring_y[None, :]
    )
    order = order.reshape(-1).astype(jnp.int32)

    carried = first_products(
        line, order, gate, up, router_weight.T, norm_gain[None, :], None, None, down
    )
    first_half, second_half = halves(behind, ahead, carried[1])
    across = [shift_mixed(first_half, True, 1), shift_mixed(second_half, True, -1)]
    for stage in ((1, 3), (2,)):
        carried = products(
            [ahead, behind] if stage == (1, 3) else across,
            order,
            stage,
            gate,
            up,
            router_weight.T,
            norm_gain[None, :],
            carried,
            select if stage == (2,) else None,
        )
    hidden, weight = carried

    low, high = down_terms(hidden, weight, order, 2, down, col_width, 2)
    low, high = shift_mixed(low, True, 1), shift_mixed(high, True, -1)
    one, three, zero = (
        down_terms(hidden, weight, order, d, down, col_width, 1)[0] for d in (1, 3, 0)
    )
    none = jnp.zeros_like(low)
    one = one.astype(F32) + jnp.concatenate([low, none], axis=1).astype(F32)
    three = three.astype(F32) + jnp.concatenate([none, high], axis=1).astype(F32)
    got = shift_mixed(one.astype(BF16), True, 1), shift_mixed(three.astype(BF16), True, -1)
    line = sum((g.astype(F32) for g in got), zero.astype(F32)).astype(BF16)
    got = [shift_mixed(line[d], False, d) for d in (1, 3, 2)]
    summed = sum((g.astype(F32) for g in got), line[0].astype(F32)).astype(BF16)
    summed = summed.reshape(SIDE, capacity, col_width)
    back = {d: shift_node(summed[at], -d) for at, d in ((1, 1), (2, 3), (3, 2))}
    returned = jnp.concatenate([summed[0]] + [back[d] for d in range(1, SIDE)], axis=0)
    expert_sum = jnp.dot(placed, returned, preferred_element_type=F32)
    return (stream + expert_sum).astype(BF16)


def solution(mesh):
    placed = (
        P(("node", "local"), "tp"),
        P("tp", "local"),
        P(("node", "tp"), "local"),
        P(),
        P(),
        P(("node", "tp"), None),
        P("node", None, ("local", "tp")),
        P("node", None, ("local", "tp")),
        P("node", ("local", "tp"), None),
    )
    return jax.shard_map(
        body, mesh=mesh, in_specs=placed, out_specs=P(("node", "tp"), "local"), check_vma=False
    )
```

```python
import functools

import jax
import jax.numpy as jnp
from jax import lax
from jax.experimental import pallas as pl
from jax.experimental.pallas import tpu as pltpu
from jax.sharding import PartitionSpec as P

SIDE = 4
PER = 1
VMEM = 8 * 1024 * 1024
F32 = jnp.float32
BF16 = jnp.bfloat16


def shift_node(value, by):
    return lax.ppermute(value, "node", [(i, (i + by) % SIDE) for i in range(SIDE)])


def shift_mixed(value, far, by):
    pairs = []
    for x in range(SIDE):
        for y in range(SIDE):
            for core in range(2):
                dx, dy = (by, 0) if (core == 0) != far else (0, by)
                to = ((x + dx) % SIDE) * SIDE + (y + dy) % SIDE
                pairs.append(((x * SIDE + y) * 2 + core, to * 2 + core))
    return lax.ppermute(value, ("local", "tp"), pairs)


def swap_core(value):
    return lax.ppermute(value, "tp", [(0, 1), (1, 0)])


EARLY_0 = [(p, dy) for dy in (1, 3) for p in range(2)]
EARLY_1 = [(1, dy) for dy in range(SIDE)]
LATE_0 = [(p, dy) for dy in (0, 2) for p in range(2)]
LATE_1 = [(0, dy) for dy in range(SIDE)]


def combine_kernel(flags, *refs):
    lows, highs, lasts, refs = refs[:3], refs[3:6], refs[6:10], refs[10:]
    early, late, residual, one_hot, tag, stream, *outs, rows, values, sems = refs
    part, width = residual.shape[1:]
    first = flags[0] == 1
    copies = []

    def block(far, near):
        if far == 2:
            return lasts[near][...]
        half = (lows if near < 2 else highs)[min(far, 2)]
        return half[near % 2 * part : (near % 2 + 1) * part, :]

    for p in range(2):
        mine = flags[1 + p] == 1
        for dy in range(SIDE):
            along_x = jnp.where(mine, block(dy, p), block(dy, p + 2))
            along_y = jnp.where(mine, block(p, dy), block(p + 2, dy))
            kept = jnp.where(first, along_x, along_y)
            at_0 = early[EARLY_1.index((p, dy))] if p == 1 else late[LATE_1.index((p, dy))]
            if dy in (1, 3):
                at_1 = early[EARLY_0.index((p, dy))]
            else:
                at_1 = late[LATE_0.index((p, dy))]
            got = jnp.where(first, at_0.astype(F32), at_1.astype(F32))
            at = flags[3 + p] * SIDE + flags[5 + dy]
            value = residual[at].astype(F32) + (kept + got)
            values[p * SIDE + dy] = value
            copy = pltpu.make_async_copy(
                values.at[p * SIDE + dy], stream.at[at], sems.at[p * SIDE + dy]
            )
            copy.start()
            copies.append(copy)
            rows[pl.ds(pl.multiple_of(at * part, part), part), :] = value.astype(BF16)
    picked = jnp.dot(one_hot[...], rows[...], preferred_element_type=F32).astype(BF16)
    for d, out in enumerate(outs):
        count = out.shape[0] - tag.shape[1]
        out[:count, :] = picked[d * count : (d + 1) * count]
        out[count:, :] = tag[d]
    for copy in copies:
        copy.wait()


def combine(flags, lows, highs, lasts, early, late, residual, one_hot, tag):
    part, width = residual.shape[1:]
    spots = one_hot.shape[0]
    operands = [in_hbm(v) for v in (*lows, *highs)] + [in_vmem(v) for v in lasts]
    operands += [in_hbm(early), in_vmem(late), in_hbm(residual), one_hot, tag]
    out_shape = [pltpu.HBM((2 * SIDE, part, width), F32)]
    out_shape += [jax.ShapeDtypeStruct((spots // SIDE + tag.shape[1], width), BF16)] * SIDE
    smem, vmem = (pl.BlockSpec(memory_space=m) for m in (pltpu.SMEM, pltpu.VMEM))
    return pl.pallas_call(
        combine_kernel,
        out_shape=out_shape,
        in_specs=[smem] + [vmem] * len(operands),
        out_specs=[pl.BlockSpec(memory_space=pl.ANY)] + [vmem] * SIDE,
        scratch_shapes=[
            pltpu.VMEM((2 * SIDE * part, width), BF16),
            pltpu.VMEM((2 * SIDE, part, width), F32),
            pltpu.SemaphoreType.DMA((2 * SIDE,)),
        ],
        compiler_params=pltpu.CompilerParams(vmem_limit_bytes=16 * 1024 * 1024),
        cost_estimate=pl.CostEstimate(
            flops=2 * spots * 2 * SIDE * part * width, bytes_accessed=1 << 22, transcendentals=0
        ),
    )(flags, *operands)


def halves(one, other, early):
    def kernel(one, other, early, first, second, sems):
        half = first.shape[0]
        copies = [
            pltpu.make_async_copy(one.at[pl.ds(0, half)], first, sems.at[0]),
            pltpu.make_async_copy(other.at[pl.ds(half, half)], second, sems.at[1]),
        ]
        for copy in copies:
            copy.start()
        for copy in copies:
            copy.wait()

    shape = jax.ShapeDtypeStruct((one.shape[0] // 2,) + one.shape[1:], one.dtype)
    anywhere = pl.BlockSpec(memory_space=pl.ANY)
    return pl.pallas_call(
        kernel,
        out_shape=[shape, shape],
        in_specs=[anywhere] * 3,
        out_specs=[anywhere] * 2,
        scratch_shapes=[pltpu.SemaphoreType.DMA((2,))],
        compiler_params=pltpu.CompilerParams(vmem_limit_bytes=1024 * 1024),
        cost_estimate=pl.CostEstimate(
            flops=0, bytes_accessed=2 * one.size * 2, transcendentals=0
        ),
    )(one, other, early)


def first_kernel(order, rows, early, *refs, first, last, features):
    weights, refs = [refs[2 * b : 2 * b + 2] for b in range(PER)], refs[2 * PER :]
    routers, refs = refs[:PER], refs[PER:]
    gains, refs = refs[:PER], refs[PER:]
    carried = None
    if not first:
        carried, refs = refs[:3], refs[3:]
    if last:
        select, hidden, weight, acc, logits, squares = refs
    else:
        acc, logits, squares = refs

    @pl.when(pl.program_id(0) == 0)
    def _():
        for at, ref in enumerate((acc, logits, squares)):
            ref[...] = jnp.zeros_like(ref) if first else carried[at][...]

    scaled = []
    for b in range(PER):
        values = rows[b].astype(F32)
        square = values * values
        for lane in range(0, values.shape[1], 128):
            squares[...] += square[:, lane : lane + 128]
        scaled.append((values * gains[b][...]).astype(BF16))
    for at in range(2):
        for core in range(2):
            total = acc[2 * at + core]
            for b in range(PER):
                total += jnp.dot(scaled[b], weights[b][at][core], preferred_element_type=F32)
            acc[2 * at + core] = total
    total = logits[...]
    for b in range(PER):
        total += lax.dot_general(
            scaled[b], routers[b][...], (((1,), (1,)), ((), ())), preferred_element_type=F32
        )
    logits[...] = total

    if last:

        @pl.when(pl.program_id(0) == pl.num_programs(0) - 1)
        def _():
            mean = jnp.sum(squares[...], axis=1, keepdims=True) / features
            scale = lax.rsqrt(mean + 1e-06)
            gap = jnp.sum(logits[...] * select[...], axis=1, keepdims=True) * scale
            weight[...] = jnp.broadcast_to(1.0 / (1.0 + jnp.exp(-gap)), weight.shape)
            for core in range(2):
                gate = acc[core] * scale
                upper = acc[2 + core] * scale
                width = gate.shape[1]
                hidden[:, core * width : (core + 1) * width] = (
                    gate / (1.0 + jnp.exp(-gate)) * upper
                ).astype(BF16)


def first_products(rows, places, gate, up, router, gain, carried, select, early):
    blocks, count, depth = rows.shape
    features, width = gate.shape[1:]
    experts = router.shape[0]
    first, last = carried is None, select is not None
    whole = lambda *shape: pl.BlockSpec(shape, lambda i, order: (0,) * len(shape))

    def weight_spec(b):
        return pl.BlockSpec((2, depth, width), lambda i, order: (0, order[i * PER + b], 0))

    def flat_spec(b, height):
        return pl.BlockSpec((height, depth), lambda i, order: (0, order[i * PER + b]))

    in_specs = [
        pl.BlockSpec((PER, count, depth), lambda i, order: (i, 0, 0)),
        pl.BlockSpec((1, 8, 128), lambda i, order: (0, 0, 0)),
    ]
    operands = [rows, in_hbm(early)]
    for b in range(PER):
        in_specs += [weight_spec(b)] * 2
        operands += [in_hbm(gate), in_hbm(up)]
    in_specs += [flat_spec(b, experts) for b in range(PER)]
    operands += [router] * PER
    in_specs += [flat_spec(b, 1) for b in range(PER)]
    operands += [gain] * PER
    sums = [(4, count, width), (count, experts), (count, 128)]
    if not first:
        in_specs += [whole(*shape) for shape in sums]
        operands += list(carried)
    scratch = []
    if last:
        in_specs.append(whole(count, experts))
        operands.append(select)
        out_shape = [
            jax.ShapeDtypeStruct((count, 2 * width), BF16),
            jax.ShapeDtypeStruct((count, 128), F32),
        ]
        scratch = [pltpu.VMEM(shape, F32) for shape in sums]
    else:
        out_shape = [jax.ShapeDtypeStruct(shape, F32) for shape in sums]
    return pl.pallas_call(
        lambda *refs: first_kernel(*refs, first=first, last=last, features=features),
        out_shape=out_shape,
        grid_spec=pltpu.PrefetchScalarGridSpec(
            num_scalar_prefetch=1,
            grid=(blocks // PER,),
            in_specs=in_specs,
            out_specs=[whole(*s.shape) for s in out_shape],
            scratch_shapes=scratch,
        ),
        compiler_params=pltpu.CompilerParams(
            dimension_semantics=("arbitrary",), vmem_limit_bytes=VMEM
        ),
        cost_estimate=pl.CostEstimate(
            flops=2 * count * depth * blocks * width * 4,
            bytes_accessed=blocks * depth * width * 8,
            transcendentals=0,
        ),
    )(places, *operands)


def in_hbm(value):
    return pltpu.with_memory_space_constraint(value, pltpu.HBM)


def in_vmem(value):
    return pltpu.with_memory_space_constraint(value, pltpu.VMEM)


def products_kernel(order, *refs, pieces, distances, last, features):
    rows, refs = refs[:pieces], refs[pieces:]
    gate, up, router, gain, *refs = refs
    carried, refs = refs[:3], refs[3:]
    if last:
        select, hidden, weight = refs
    else:
        acc, logits, squares = refs
    count, depth = rows[0].shape[1:]
    width = gate.shape[2]
    scaled, spans = [], []
    square_sum = carried[2][...]
    arrived = [(ref, at) for ref in rows for at in range(ref.shape[0])]
    for b, (ref, at) in enumerate(arrived):
        block = order[distances[b // SIDE] * SIDE + b % SIDE]
        span = pl.ds(pl.multiple_of(block * depth, depth), depth)
        values = ref[at].astype(F32)
        square = values * values
        for lane in range(0, depth, 128):
            square_sum += square[:, lane : lane + 128]
        scaled.append((values * gain[:, span]).astype(BF16))
        spans.append(span)
    totals = []
    for at, matrix in enumerate((gate, up)):
        for core in range(2):
            total = carried[0][2 * at + core]
            for values, span in zip(scaled, spans):
                total += jnp.dot(values, matrix[core, span, :], preferred_element_type=F32)
            if last:
                totals.append(total)
            else:
                acc[2 * at + core] = total
    total = carried[1][...]
    for values, span in zip(scaled, spans):
        total += lax.dot_general(
            values, router[:, span], (((1,), (1,)), ((), ())), preferred_element_type=F32
        )
    if not last:
        logits[...] = total
        squares[...] = square_sum
        return
    mean = jnp.sum(square_sum, axis=1, keepdims=True) / features
    scale = lax.rsqrt(mean + 1e-06)
    gap = jnp.sum(total * select[...], axis=1, keepdims=True) * scale
    weight[...] = jnp.broadcast_to(1.0 / (1.0 + jnp.exp(-gap)), weight.shape)
    for core in range(2):
        gated = totals[core] * scale
        upper = totals[2 + core] * scale
        hidden[:, core * width : (core + 1) * width] = (
            gated / (1.0 + jnp.exp(-gated)) * upper
        ).astype(BF16)


def local_call(kernel, places, operands, out_shape, flops, touched):
    smem, vmem = (pl.BlockSpec(memory_space=m) for m in (pltpu.SMEM, pltpu.VMEM))
    return pl.pallas_call(
        kernel,
        out_shape=out_shape,
        in_specs=[smem] + [vmem] * len(operands),
        out_specs=jax.tree.map(lambda _: vmem, out_shape),
        compiler_params=pltpu.CompilerParams(vmem_limit_bytes=VMEM),
        cost_estimate=pl.CostEstimate(flops=flops, bytes_accessed=touched, transcendentals=0),
    )(places, *operands)


def products(rows, places, distances, gate, up, router, gain, carried, select):
    count, depth = rows[0].shape[1:]
    blocks = SIDE * len(distances)
    features, width = gate.shape[1:]
    last = select is not None
    operands = [*rows, in_vmem(gate), in_vmem(up), router, gain, *map(in_vmem, carried)]
    if last:
        operands.append(select)
        out_shape = [
            jax.ShapeDtypeStruct((count, 2 * width), BF16),
            jax.ShapeDtypeStruct((count, 128), F32),
        ]
    else:
        sums = [(4, count, width), (count, router.shape[0]), (count, 128)]
        out_shape = [jax.ShapeDtypeStruct(shape, F32) for shape in sums]
    return local_call(
        lambda *refs: products_kernel(
            *refs, pieces=len(rows), distances=distances, last=last, features=features
        ),
        places,
        operands,
        out_shape,
        2 * count * depth * blocks * width * 4,
        blocks * depth * width * 8,
    )


def down_kernel(order, hidden, weight, down, *outs, distance):
    width, depth = hidden.shape[1] // 2, outs[0].shape[2]
    for b in range(SIDE):
        span = pl.ds(pl.multiple_of(order[distance * SIDE + b] * depth, depth), depth)
        term = jnp.dot(hidden[:, :width], down[0, :, span], preferred_element_type=F32)
        term += jnp.dot(hidden[:, width:], down[1, :, span], preferred_element_type=F32)
        term = (term * weight[:, :1]).astype(BF16)
        for at, out in enumerate(outs):
            out[b] = term[at * out.shape[1] : (at + 1) * out.shape[1]]


def down_terms(hidden, weight, places, distance, down, depth, parts):
    count, both = hidden.shape
    return local_call(
        functools.partial(down_kernel, distance=distance),
        places,
        [hidden, weight, in_vmem(down)],
        [jax.ShapeDtypeStruct((SIDE, count // parts, depth), BF16)] * parts,
        2 * count * both * depth * SIDE,
        both * depth * SIDE * 2,
    )


def body(
    mixer_out,
    out_proj,
    residual,
    norm_gain,
    router_weight,
    expert_ids,
    expert_gate,
    expert_up,
    expert_down,
):
    node = lax.axis_index("node")
    local = lax.axis_index("local")
    core = lax.axis_index("tp")
    x, y = local // SIDE, local % SIDE
    half_rows, col_width = residual.shape
    capacity = half_rows // 16
    spots = SIDE * capacity
    part = mixer_out.shape[0]

    gate, up, down = (
        lax.all_gather(w, "tp", axis=0, tiled=True) for w in (expert_gate, expert_up, expert_down)
    )

    first, partner = expert_ids[:, 0], expert_ids[:, 1]
    routed = first < SIDE
    relative = lax.rem(first - node + SIDE, SIDE)
    marks = (routed[:, None] & (relative[:, None] == jnp.arange(SIDE)[None, :])).astype(jnp.int32)
    slots = jnp.sum((jnp.cumsum(marks, axis=0) - marks) * marks, axis=1)
    spot = jnp.where(routed, relative * capacity + slots, -1)
    placed = (spot[:, None] == jnp.arange(spots)[None, :]).astype(BF16)
    picked = spot[None, :] == jnp.arange(spots)[:, None]
    partners = jnp.sum(jnp.where(picked, partner[None, :], 0), axis=1).reshape(SIDE, capacity)
    mine = [((x + p) % SIDE) // 2 == core for p in range(2)]

    flags = [core == 0] + mine + [(x + p) % 2 for p in range(2)] + [(y + dy) % SIDE for dy in range(SIDE)]
    flags = jnp.stack([f.astype(jnp.int32) for f in flags])

    ahead, behind = shift_mixed(mixer_out, False, -1), shift_mixed(mixer_out, False, 1)
    across = [
        shift_mixed(behind[: part // 2], False, 1),
        shift_mixed(ahead[part // 2 :], False, -1),
    ]
    low = jnp.concatenate([mixer_out, ahead], axis=0)
    low_1, low_3 = shift_mixed(low, True, -1), shift_mixed(low, True, 1)
    high = jnp.concatenate(across + [behind], axis=0)
    high_1, high_3 = shift_mixed(high, True, -1), shift_mixed(high, True, 1)
    far_2 = []
    for behind, ahead in ((low_3, low_1), (high_3, high_1)):
        first_half, second_half = halves(behind, ahead, flags)
        far_2 += [shift_mixed(first_half, True, 1), shift_mixed(second_half, True, -1)]

    def project(rows):
        return lax.optimization_barrier(jnp.dot(rows, out_proj, preferred_element_type=F32))

    lows = {far: project(rows) for far, rows in ((0, low), (1, low_1), (3, low_3))}
    highs = {far: project(rows) for far, rows in ((0, high), (1, high_1), (3, high_3))}
    lasts = [project(rows) for rows in far_2]

    def block(far, near):
        if far == 2:
            return lasts[near]
        half = (lows if near < 2 else highs)[far]
        return half[near % 2 * part : (near % 2 + 1) * part]

    def sent(names_0, names_1):
        out = []
        for (p, dy), (q, ey) in zip(names_0, names_1):
            along_x = jnp.where(mine[p], block(dy, p + 2), block(dy, p))
            along_y = jnp.where(mine[q], block(q + 2, ey), block(q, ey))
            out.append(jnp.where(core == 0, along_x, along_y))
        return jnp.stack(out).astype(BF16)

    got_early, got_late = swap_core(sent(EARLY_0, EARLY_1)), swap_core(sent(LATE_0, LATE_1))
    tag = jnp.zeros((SIDE, 16, col_width), BF16).at[:, 0, :capacity].set(partners.astype(BF16))
    stream, *bucket = combine(
        flags,
        [lows[far] for far in (0, 1, 3)],
        [highs[far] for far in (0, 1, 3)],
        lasts,
        got_early,
        got_late,
        residual.reshape(2 * SIDE, part, col_width),
        picked.astype(BF16),
        tag,
    )
    stream = stream.reshape(half_rows, col_width)

    landed = [bucket[0]] + [shift_node(bucket[d], d) for d in (1, 3, 2)]
    partners = jnp.concatenate([v[capacity, :capacity] for v in landed]).astype(jnp.int32)
    landed = jnp.concatenate([v[:capacity] for v in landed], axis=0)
    experts = jnp.arange(router_weight.shape[1])[None, :]
    select = (experts == node).astype(F32) - (experts == partners[:, None]).astype(F32)
    got = {(-d) % SIDE: shift_mixed(landed, False, d) for d in (1, 3, 2)}
    line = jnp.stack([landed] + [got[d] for d in range(1, SIDE)], axis=0)
    ahead, behind = shift_mixed(line, True, -1), shift_mixed(line, True, 1)
    ring_x = ((x + jnp.arange(SIDE)) % SIDE) * SIDE
    ring_y = (y + jnp.arange(SIDE)) % SIDE
    order = jnp.where(
        core == 0, ring_x[None, :] + ring_y[:, None], ring_x[:, None] + ring_y[None, :]
    )
    order = order.reshape(-1).astype(jnp.int32)

    carried = first_products(
        line, order, gate, up, router_weight.T, norm_gain[None, :], None, None, down
    )
    first_half, second_half = halves(behind, ahead, carried[1])
    across = [shift_mixed(first_half, True, 1), shift_mixed(second_half, True, -1)]
    for stage in ((1, 3), (2,)):
        carried = products(
            [ahead, behind] if stage == (1, 3) else across,
            order,
            stage,
            gate,
            up,
            router_weight.T,
            norm_gain[None, :],
            carried,
            select if stage == (2,) else None,
        )
    hidden, weight = carried

    low, high = down_terms(hidden, weight, order, 2, down, col_width, 2)
    low, high = shift_mixed(low, True, 1), shift_mixed(high, True, -1)
    one, three, zero = (
        down_terms(hidden, weight, order, d, down, col_width, 1)[0] for d in (1, 3, 0)
    )
    none = jnp.zeros_like(low)
    one = one.astype(F32) + jnp.concatenate([low, none], axis=1).astype(F32)
    three = three.astype(F32) + jnp.concatenate([none, high], axis=1).astype(F32)
    got = shift_mixed(one.astype(BF16), True, 1), shift_mixed(three.astype(BF16), True, -1)
    line = sum((g.astype(F32) for g in got), zero.astype(F32)).astype(BF16)
    got = [shift_mixed(line[d], False, d) for d in (1, 3, 2)]
    summed = sum((g.astype(F32) for g in got), line[0].astype(F32)).astype(BF16)
    summed = summed.reshape(SIDE, capacity, col_width)
    back = {d: shift_node(summed[at], -d) for at, d in ((1, 1), (2, 3), (3, 2))}
    returned = jnp.concatenate([summed[0]] + [back[d] for d in range(1, SIDE)], axis=0)
    expert_sum = jnp.dot(placed, returned, preferred_element_type=F32)
    return (stream + expert_sum).astype(BF16)


def solution(mesh):
    placed = (
        P(("node", "local"), "tp"),
        P("tp", "local"),
        P(("node", "tp"), "local"),
        P(),
        P(),
        P(("node", "tp"), None),
        P("node", None, ("local", "tp")),
        P("node", None, ("local", "tp")),
        P("node", ("local", "tp"), None),
    )
    return jax.shard_map(
        body, mesh=mesh, in_specs=placed, out_specs=P(("node", "tp"), "local"), check_vma=False
    )
```

```python
import functools

import jax
import jax.numpy as jnp
from jax import lax
from jax.experimental import pallas as pl
from jax.experimental.pallas import tpu as pltpu
from jax.sharding import PartitionSpec as P

SIDE = 4
PER = 1
VMEM = 8 * 1024 * 1024
F32 = jnp.float32
BF16 = jnp.bfloat16


def shift_node(value, by):
    return lax.ppermute(value, "node", [(i, (i + by) % SIDE) for i in range(SIDE)])


def shift_mixed(value, far, by):
    pairs = []
    for x in range(SIDE):
        for y in range(SIDE):
            for core in range(2):
                dx, dy = (by, 0) if (core == 0) != far else (0, by)
                to = ((x + dx) % SIDE) * SIDE + (y + dy) % SIDE
                pairs.append(((x * SIDE + y) * 2 + core, to * 2 + core))
    return lax.ppermute(value, ("local", "tp"), pairs)


def swap_core(value):
    return lax.ppermute(value, "tp", [(0, 1), (1, 0)])


EARLY_0 = [(p, dy) for dy in (1, 3) for p in range(2)]
EARLY_1 = [(1, dy) for dy in range(SIDE)]
LATE_0 = [(p, dy) for dy in (0, 2) for p in range(2)]
LATE_1 = [(0, dy) for dy in range(SIDE)]


def combine_kernel(flags, *refs):
    lows, highs, lasts, refs = refs[:3], refs[3:6], refs[6:10], refs[10:]
    early, late, residual, one_hot, tag, stream, *outs, rows, values, sems = refs
    part, width = residual.shape[1:]
    first = flags[0] == 1
    copies = []

    def block(far, near):
        if far == 2:
            return lasts[near][...]
        half = (lows if near < 2 else highs)[min(far, 2)]
        return half[near % 2 * part : (near % 2 + 1) * part, :]

    for p in range(2):
        mine = flags[1 + p] == 1
        for dy in range(SIDE):
            along_x = jnp.where(mine, block(dy, p), block(dy, p + 2))
            along_y = jnp.where(mine, block(p, dy), block(p + 2, dy))
            kept = jnp.where(first, along_x, along_y)
            at_0 = early[EARLY_1.index((p, dy))] if p == 1 else late[LATE_1.index((p, dy))]
            if dy in (1, 3):
                at_1 = early[EARLY_0.index((p, dy))]
            else:
                at_1 = late[LATE_0.index((p, dy))]
            got = jnp.where(first, at_0.astype(F32), at_1.astype(F32))
            at = flags[3 + p] * SIDE + flags[5 + dy]
            value = residual[at].astype(F32) + (kept + got)
            values[p * SIDE + dy] = value
            copy = pltpu.make_async_copy(
                values.at[p * SIDE + dy], stream.at[at], sems.at[p * SIDE + dy]
            )
            copy.start()
            copies.append(copy)
            rows[pl.ds(pl.multiple_of(at * part, part), part), :] = value.astype(BF16)
    picked = jnp.dot(one_hot[...], rows[...], preferred_element_type=F32).astype(BF16)
    for d, out in enumerate(outs):
        count = out.shape[0] - tag.shape[1]
        out[:count, :] = picked[d * count : (d + 1) * count]
        out[count:, :] = tag[d]
    for copy in copies:
        copy.wait()


def combine(flags, lows, highs, lasts, early, late, residual, one_hot, tag):
    part, width = residual.shape[1:]
    spots = one_hot.shape[0]
    operands = [in_hbm(v) for v in (*lows, *highs)] + [in_vmem(v) for v in lasts]
    operands += [in_hbm(early), in_vmem(late), in_hbm(residual), one_hot, tag]
    out_shape = [pltpu.HBM((2 * SIDE, part, width), F32)]
    out_shape += [jax.ShapeDtypeStruct((spots // SIDE + tag.shape[1], width), BF16)] * SIDE
    smem, vmem = (pl.BlockSpec(memory_space=m) for m in (pltpu.SMEM, pltpu.VMEM))
    return pl.pallas_call(
        combine_kernel,
        out_shape=out_shape,
        in_specs=[smem] + [vmem] * len(operands),
        out_specs=[pl.BlockSpec(memory_space=pl.ANY)] + [vmem] * SIDE,
        scratch_shapes=[
            pltpu.VMEM((2 * SIDE * part, width), BF16),
            pltpu.VMEM((2 * SIDE, part, width), F32),
            pltpu.SemaphoreType.DMA((2 * SIDE,)),
        ],
        compiler_params=pltpu.CompilerParams(vmem_limit_bytes=16 * 1024 * 1024),
        cost_estimate=pl.CostEstimate(
            flops=2 * spots * 2 * SIDE * part * width, bytes_accessed=1 << 22, transcendentals=0
        ),
    )(flags, *operands)


def halves(one, other, early, cut=2):
    def kernel(one, other, early, first, second, sems):
        half = first.shape[0]
        copies = [
            pltpu.make_async_copy(one.at[pl.ds(0, half)], first, sems.at[0]),
            pltpu.make_async_copy(other.at[pl.ds(other.shape[0] - half, half)], second, sems.at[1]),
        ]
        for copy in copies:
            copy.start()
        for copy in copies:
            copy.wait()

    shape = jax.ShapeDtypeStruct((one.shape[0] // cut,) + one.shape[1:], one.dtype)
    anywhere = pl.BlockSpec(memory_space=pl.ANY)
    return pl.pallas_call(
        kernel,
        out_shape=[shape, shape],
        in_specs=[anywhere] * 3,
        out_specs=[anywhere] * 2,
        scratch_shapes=[pltpu.SemaphoreType.DMA((2,))],
        compiler_params=pltpu.CompilerParams(vmem_limit_bytes=1024 * 1024),
        cost_estimate=pl.CostEstimate(
            flops=0, bytes_accessed=2 * one.size * 2, transcendentals=0
        ),
    )(one, other, early)


def first_kernel(order, rows, early, *refs, first, last, features):
    weights, refs = [refs[2 * b : 2 * b + 2] for b in range(PER)], refs[2 * PER :]
    routers, refs = refs[:PER], refs[PER:]
    gains, refs = refs[:PER], refs[PER:]
    carried = None
    if not first:
        carried, refs = refs[:3], refs[3:]
    if last:
        select, hidden, weight, acc, logits, squares = refs
    else:
        acc, logits, squares = refs

    @pl.when(pl.program_id(0) == 0)
    def _():
        for at, ref in enumerate((acc, logits, squares)):
            ref[...] = jnp.zeros_like(ref) if first else carried[at][...]

    scaled = []
    for b in range(PER):
        values = rows[b].astype(F32)
        square = values * values
        for lane in range(0, values.shape[1], 128):
            squares[...] += square[:, lane : lane + 128]
        scaled.append((values * gains[b][...]).astype(BF16))
    for at in range(2):
        for core in range(2):
            total = acc[2 * at + core]
            for b in range(PER):
                total += jnp.dot(scaled[b], weights[b][at][core], preferred_element_type=F32)
            acc[2 * at + core] = total
    total = logits[...]
    for b in range(PER):
        total += lax.dot_general(
            scaled[b], routers[b][...], (((1,), (1,)), ((), ())), preferred_element_type=F32
        )
    logits[...] = total

    if last:

        @pl.when(pl.program_id(0) == pl.num_programs(0) - 1)
        def _():
            mean = jnp.sum(squares[...], axis=1, keepdims=True) / features
            scale = lax.rsqrt(mean + 1e-06)
            gap = jnp.sum(logits[...] * select[...], axis=1, keepdims=True) * scale
            weight[...] = jnp.broadcast_to(1.0 / (1.0 + jnp.exp(-gap)), weight.shape)
            for core in range(2):
                gate = acc[core] * scale
                upper = acc[2 + core] * scale
                width = gate.shape[1]
                hidden[:, core * width : (core + 1) * width] = (
                    gate / (1.0 + jnp.exp(-gate)) * upper
                ).astype(BF16)


def first_products(rows, places, gate, up, router, gain, carried, select, early):
    blocks, count, depth = rows.shape
    features, width = gate.shape[1:]
    experts = router.shape[0]
    first, last = carried is None, select is not None
    whole = lambda *shape: pl.BlockSpec(shape, lambda i, order: (0,) * len(shape))

    def weight_spec(b):
        return pl.BlockSpec((2, depth, width), lambda i, order: (0, order[i * PER + b], 0))

    def flat_spec(b, height):
        return pl.BlockSpec((height, depth), lambda i, order: (0, order[i * PER + b]))

    in_specs = [
        pl.BlockSpec((PER, count, depth), lambda i, order: (i, 0, 0)),
        pl.BlockSpec((1, 8, 128), lambda i, order: (0, 0, 0)),
    ]
    operands = [rows, in_hbm(early)]
    for b in range(PER):
        in_specs += [weight_spec(b)] * 2
        operands += [in_hbm(gate), in_hbm(up)]
    in_specs += [flat_spec(b, experts) for b in range(PER)]
    operands += [router] * PER
    in_specs += [flat_spec(b, 1) for b in range(PER)]
    operands += [gain] * PER
    sums = [(4, count, width), (count, experts), (count, 128)]
    if not first:
        in_specs += [whole(*shape) for shape in sums]
        operands += list(carried)
    scratch = []
    if last:
        in_specs.append(whole(count, experts))
        operands.append(select)
        out_shape = [
            jax.ShapeDtypeStruct((count, 2 * width), BF16),
            jax.ShapeDtypeStruct((count, 128), F32),
        ]
        scratch = [pltpu.VMEM(shape, F32) for shape in sums]
    else:
        out_shape = [jax.ShapeDtypeStruct(shape, F32) for shape in sums]
    return pl.pallas_call(
        lambda *refs: first_kernel(*refs, first=first, last=last, features=features),
        out_shape=out_shape,
        grid_spec=pltpu.PrefetchScalarGridSpec(
            num_scalar_prefetch=1,
            grid=(blocks // PER,),
            in_specs=in_specs,
            out_specs=[whole(*s.shape) for s in out_shape],
            scratch_shapes=scratch,
        ),
        compiler_params=pltpu.CompilerParams(
            dimension_semantics=("arbitrary",), vmem_limit_bytes=VMEM
        ),
        cost_estimate=pl.CostEstimate(
            flops=2 * count * depth * blocks * width * 4,
            bytes_accessed=blocks * depth * width * 8,
            transcendentals=0,
        ),
    )(places, *operands)


def in_hbm(value):
    return pltpu.with_memory_space_constraint(value, pltpu.HBM)


def in_vmem(value):
    return pltpu.with_memory_space_constraint(value, pltpu.VMEM)


def products_kernel(order, *refs, pieces, distances, last, features):
    rows, refs = refs[:pieces], refs[pieces:]
    gate, up, router, gain, *refs = refs
    carried, refs = refs[:3], refs[3:]
    if last:
        select, hidden, weight = refs
    else:
        acc, logits, squares = refs
    count, depth = rows[0].shape[1:]
    width = gate.shape[2]
    scaled, spans = [], []
    square_sum = carried[2][...]
    arrived = [(ref, at) for ref in rows for at in range(ref.shape[0])]
    for b, (ref, at) in enumerate(arrived):
        block = order[distances[b // SIDE] * SIDE + b % SIDE]
        span = pl.ds(pl.multiple_of(block * depth, depth), depth)
        values = ref[at].astype(F32)
        square = values * values
        for lane in range(0, depth, 128):
            square_sum += square[:, lane : lane + 128]
        scaled.append((values * gain[:, span]).astype(BF16))
        spans.append(span)
    totals = []
    for at, matrix in enumerate((gate, up)):
        for core in range(2):
            total = carried[0][2 * at + core]
            for values, span in zip(scaled, spans):
                total += jnp.dot(values, matrix[core, span, :], preferred_element_type=F32)
            if last:
                totals.append(total)
            else:
                acc[2 * at + core] = total
    total = carried[1][...]
    for values, span in zip(scaled, spans):
        total += lax.dot_general(
            values, router[:, span], (((1,), (1,)), ((), ())), preferred_element_type=F32
        )
    if not last:
        logits[...] = total
        squares[...] = square_sum
        return
    mean = jnp.sum(square_sum, axis=1, keepdims=True) / features
    scale = lax.rsqrt(mean + 1e-06)
    gap = jnp.sum(total * select[...], axis=1, keepdims=True) * scale
    weight[...] = jnp.broadcast_to(1.0 / (1.0 + jnp.exp(-gap)), weight.shape)
    for core in range(2):
        gated = totals[core] * scale
        upper = totals[2 + core] * scale
        hidden[:, core * width : (core + 1) * width] = (
            gated / (1.0 + jnp.exp(-gated)) * upper
        ).astype(BF16)


def local_call(kernel, places, operands, out_shape, flops, touched):
    smem, vmem = (pl.BlockSpec(memory_space=m) for m in (pltpu.SMEM, pltpu.VMEM))
    return pl.pallas_call(
        kernel,
        out_shape=out_shape,
        in_specs=[smem] + [vmem] * len(operands),
        out_specs=jax.tree.map(lambda _: vmem, out_shape),
        compiler_params=pltpu.CompilerParams(vmem_limit_bytes=VMEM),
        cost_estimate=pl.CostEstimate(flops=flops, bytes_accessed=touched, transcendentals=0),
    )(places, *operands)


def products(rows, places, distances, gate, up, router, gain, carried, select):
    count, depth = rows[0].shape[1:]
    blocks = SIDE * len(distances)
    features, width = gate.shape[1:]
    last = select is not None
    operands = [*rows, in_vmem(gate), in_vmem(up), router, gain, *map(in_vmem, carried)]
    if last:
        operands.append(select)
        out_shape = [
            jax.ShapeDtypeStruct((count, 2 * width), BF16),
            jax.ShapeDtypeStruct((count, 128), F32),
        ]
    else:
        sums = [(4, count, width), (count, router.shape[0]), (count, 128)]
        out_shape = [jax.ShapeDtypeStruct(shape, F32) for shape in sums]
    return local_call(
        lambda *refs: products_kernel(
            *refs, pieces=len(rows), distances=distances, last=last, features=features
        ),
        places,
        operands,
        out_shape,
        2 * count * depth * blocks * width * 4,
        blocks * depth * width * 8,
    )


def down_kernel(order, hidden, weight, down, *outs, distance):
    width, depth = hidden.shape[1] // 2, outs[0].shape[2]
    for b in range(SIDE):
        span = pl.ds(pl.multiple_of(order[distance * SIDE + b] * depth, depth), depth)
        term = jnp.dot(hidden[:, :width], down[0, :, span], preferred_element_type=F32)
        term += jnp.dot(hidden[:, width:], down[1, :, span], preferred_element_type=F32)
        term = (term * weight[:, :1]).astype(BF16)
        for at, out in enumerate(outs):
            out[b] = term[at * out.shape[1] : (at + 1) * out.shape[1]]


def down_terms(hidden, weight, places, distance, down, depth, parts):
    count, both = hidden.shape
    return local_call(
        functools.partial(down_kernel, distance=distance),
        places,
        [hidden, weight, in_vmem(down)],
        [jax.ShapeDtypeStruct((SIDE, count // parts, depth), BF16)] * parts,
        2 * count * both * depth * SIDE,
        both * depth * SIDE * 2,
    )


def body(
    mixer_out,
    out_proj,
    residual,
    norm_gain,
    router_weight,
    expert_ids,
    expert_gate,
    expert_up,
    expert_down,
):
    node = lax.axis_index("node")
    local = lax.axis_index("local")
    core = lax.axis_index("tp")
    x, y = local // SIDE, local % SIDE
    half_rows, col_width = residual.shape
    capacity = half_rows // 16
    spots = SIDE * capacity
    part = mixer_out.shape[0]

    gate, up, down = (
        lax.all_gather(w, "tp", axis=0, tiled=True) for w in (expert_gate, expert_up, expert_down)
    )

    first, partner = expert_ids[:, 0], expert_ids[:, 1]
    routed = first < SIDE
    relative = lax.rem(first - node + SIDE, SIDE)
    marks = (routed[:, None] & (relative[:, None] == jnp.arange(SIDE)[None, :])).astype(jnp.int32)
    slots = jnp.sum((jnp.cumsum(marks, axis=0) - marks) * marks, axis=1)
    spot = jnp.where(routed, relative * capacity + slots, -1)
    placed = (spot[:, None] == jnp.arange(spots)[None, :]).astype(BF16)
    picked = spot[None, :] == jnp.arange(spots)[:, None]
    partners = jnp.sum(jnp.where(picked, partner[None, :], 0), axis=1).reshape(SIDE, capacity)
    mine = [((x + p) % SIDE) // 2 == core for p in range(2)]

    flags = [core == 0] + mine + [(x + p) % 2 for p in range(2)] + [(y + dy) % SIDE for dy in range(SIDE)]
    flags = jnp.stack([f.astype(jnp.int32) for f in flags])

    ahead, behind = shift_mixed(mixer_out, False, -1), shift_mixed(mixer_out, False, 1)
    across = [
        shift_mixed(behind[: part // 2], False, 1),
        shift_mixed(ahead[part // 2 :], False, -1),
    ]
    low = jnp.concatenate([mixer_out, ahead], axis=0)
    low_1, low_3 = shift_mixed(low, True, -1), shift_mixed(low, True, 1)
    high = jnp.concatenate(across + [behind], axis=0)
    high_1, high_3 = shift_mixed(high, True, -1), shift_mixed(high, True, 1)
    far_2 = []
    for behind, ahead in ((low_3, low_1), (high_3, high_1)):
        first_half, second_half = halves(behind, ahead, flags)
        far_2 += [shift_mixed(first_half, True, 1), shift_mixed(second_half, True, -1)]

    def project(rows):
        return lax.optimization_barrier(jnp.dot(rows, out_proj, preferred_element_type=F32))

    lows = {far: project(rows) for far, rows in ((0, low), (1, low_1), (3, low_3))}
    highs = {far: project(rows) for far, rows in ((0, high), (1, high_1), (3, high_3))}
    lasts = [project(rows) for rows in far_2]

    def block(far, near):
        if far == 2:
            return lasts[near]
        half = (lows if near < 2 else highs)[far]
        return half[near % 2 * part : (near % 2 + 1) * part]

    def sent(names_0, names_1):
        out = []
        for (p, dy), (q, ey) in zip(names_0, names_1):
            along_x = jnp.where(mine[p], block(dy, p + 2), block(dy, p))
            along_y = jnp.where(mine[q], block(q + 2, ey), block(q, ey))
            out.append(jnp.where(core == 0, along_x, along_y))
        return jnp.stack(out).astype(BF16)

    got_early, got_late = swap_core(sent(EARLY_0, EARLY_1)), swap_core(sent(LATE_0, LATE_1))
    tag = jnp.zeros((SIDE, 16, col_width), BF16).at[:, 0, :capacity].set(partners.astype(BF16))
    stream, *bucket = combine(
        flags,
        [lows[far] for far in (0, 1, 3)],
        [highs[far] for far in (0, 1, 3)],
        lasts,
        got_early,
        got_late,
        residual.reshape(2 * SIDE, part, col_width),
        picked.astype(BF16),
        tag,
    )
    stream = stream.reshape(half_rows, col_width)

    landed = [bucket[0]] + [shift_node(bucket[d], d) for d in (1, 3, 2)]
    partners = jnp.concatenate([v[capacity, :capacity] for v in landed]).astype(jnp.int32)
    landed = jnp.concatenate([v[:capacity] for v in landed], axis=0)
    experts = jnp.arange(router_weight.shape[1])[None, :]
    select = (experts == node).astype(F32) - (experts == partners[:, None]).astype(F32)
    got = {(-d) % SIDE: shift_mixed(landed, False, d) for d in (1, 3, 2)}
    line_a, line_b = jnp.stack([landed, got[1]]), jnp.stack([got[2], got[3]])
    behind_a, ahead_b = shift_mixed(line_a, True, 1), shift_mixed(line_b, True, -1)
    behind_b, ahead_a = shift_mixed(line_b, True, 1), shift_mixed(line_a, True, -1)
    line = jnp.concatenate([line_a, line_b], axis=0)
    ring_x = ((x + jnp.arange(SIDE)) % SIDE) * SIDE
    ring_y = (y + jnp.arange(SIDE)) % SIDE
    order = jnp.where(
        core == 0, ring_x[None, :] + ring_y[:, None], ring_x[:, None] + ring_y[None, :]
    )
    order = order.reshape(-1).astype(jnp.int32)

    carried = first_products(
        line, order, gate, up, router_weight.T, norm_gain[None, :], None, None, down
    )
    first_half, second_half = halves(behind_a, ahead_b, carried[1], 1)
    across = [shift_mixed(first_half, True, 1), shift_mixed(second_half, True, -1)]
    for stage in ((1, 3), (2,)):
        carried = products(
            [ahead_a, ahead_b, behind_a, behind_b] if stage == (1, 3) else across,
            order,
            stage,
            gate,
            up,
            router_weight.T,
            norm_gain[None, :],
            carried,
            select if stage == (2,) else None,
        )
    hidden, weight = carried

    low, high = down_terms(hidden, weight, order, 2, down, col_width, 2)
    low, high = shift_mixed(low, True, 1), shift_mixed(high, True, -1)
    one, three, zero = (
        down_terms(hidden, weight, order, d, down, col_width, 1)[0] for d in (1, 3, 0)
    )
    none = jnp.zeros_like(low)
    one = one.astype(F32) + jnp.concatenate([low, none], axis=1).astype(F32)
    three = three.astype(F32) + jnp.concatenate([none, high], axis=1).astype(F32)
    got = shift_mixed(one.astype(BF16), True, 1), shift_mixed(three.astype(BF16), True, -1)
    line = sum((g.astype(F32) for g in got), zero.astype(F32)).astype(BF16)
    got = [shift_mixed(line[d], False, d) for d in (1, 3, 2)]
    summed = sum((g.astype(F32) for g in got), line[0].astype(F32)).astype(BF16)
    summed = summed.reshape(SIDE, capacity, col_width)
    back = {d: shift_node(summed[at], -d) for at, d in ((1, 1), (2, 3), (3, 2))}
    returned = jnp.concatenate([summed[0]] + [back[d] for d in range(1, SIDE)], axis=0)
    expert_sum = jnp.dot(placed, returned, preferred_element_type=F32)
    return (stream + expert_sum).astype(BF16)


def solution(mesh):
    placed = (
        P(("node", "local"), "tp"),
        P("tp", "local"),
        P(("node", "tp"), "local"),
        P(),
        P(),
        P(("node", "tp"), None),
        P("node", None, ("local", "tp")),
        P("node", None, ("local", "tp")),
        P("node", ("local", "tp"), None),
    )
    return jax.shard_map(
        body, mesh=mesh, in_specs=placed, out_specs=P(("node", "tp"), "local"), check_vma=False
    )
```

```python
import functools

import jax
import jax.numpy as jnp
from jax import lax
from jax.experimental import pallas as pl
from jax.experimental.pallas import tpu as pltpu
from jax.sharding import PartitionSpec as P

SIDE = 4
PER = 2
VMEM = 8 * 1024 * 1024
F32 = jnp.float32
BF16 = jnp.bfloat16


def shift_node(value, by):
    return lax.ppermute(value, "node", [(i, (i + by) % SIDE) for i in range(SIDE)])


def shift_mixed(value, far, by):
    pairs = []
    for x in range(SIDE):
        for y in range(SIDE):
            for core in range(2):
                dx, dy = (by, 0) if (core == 0) != far else (0, by)
                to = ((x + dx) % SIDE) * SIDE + (y + dy) % SIDE
                pairs.append(((x * SIDE + y) * 2 + core, to * 2 + core))
    return lax.ppermute(value, ("local", "tp"), pairs)


def swap_core(value):
    return lax.ppermute(value, "tp", [(0, 1), (1, 0)])


EARLY_0 = [(p, dy) for dy in (1, 3) for p in range(2)]
EARLY_1 = [(1, dy) for dy in range(SIDE)]
LATE_0 = [(p, dy) for dy in (0, 2) for p in range(2)]
LATE_1 = [(0, dy) for dy in range(SIDE)]


def combine_kernel(flags, *refs):
    lows, highs, lasts, refs = refs[:3], refs[3:6], refs[6:10], refs[10:]
    early, late, residual, one_hot, tag, stream, *outs, rows, values, sems = refs
    part, width = residual.shape[1:]
    first = flags[0] == 1
    copies = []

    def block(far, near):
        if far == 2:
            return lasts[near][...]
        half = (lows if near < 2 else highs)[min(far, 2)]
        return half[near % 2 * part : (near % 2 + 1) * part, :]

    for p in range(2):
        mine = flags[1 + p] == 1
        for dy in range(SIDE):
            along_x = jnp.where(mine, block(dy, p), block(dy, p + 2))
            along_y = jnp.where(mine, block(p, dy), block(p + 2, dy))
            kept = jnp.where(first, along_x, along_y)
            at_0 = early[EARLY_1.index((p, dy))] if p == 1 else late[LATE_1.index((p, dy))]
            if dy in (1, 3):
                at_1 = early[EARLY_0.index((p, dy))]
            else:
                at_1 = late[LATE_0.index((p, dy))]
            got = jnp.where(first, at_0.astype(F32), at_1.astype(F32))
            at = flags[3 + p] * SIDE + flags[5 + dy]
            value = residual[at].astype(F32) + (kept + got)
            values[p * SIDE + dy] = value
            copy = pltpu.make_async_copy(
                values.at[p * SIDE + dy], stream.at[at], sems.at[p * SIDE + dy]
            )
            copy.start()
            copies.append(copy)
            rows[pl.ds(pl.multiple_of(at * part, part), part), :] = value.astype(BF16)
    picked = jnp.dot(one_hot[...], rows[...], preferred_element_type=F32).astype(BF16)
    for d, out in enumerate(outs):
        count = out.shape[0] - tag.shape[1]
        out[:count, :] = picked[d * count : (d + 1) * count]
        out[count:, :] = tag[d]
    for copy in copies:
        copy.wait()


def combine(flags, lows, highs, lasts, early, late, residual, one_hot, tag):
    part, width = residual.shape[1:]
    spots = one_hot.shape[0]
    operands = [in_hbm(v) for v in (*lows, *highs)] + [in_vmem(v) for v in lasts]
    operands += [in_hbm(early), in_vmem(late), in_hbm(residual), one_hot, tag]
    out_shape = [pltpu.HBM((2 * SIDE, part, width), F32)]
    out_shape += [jax.ShapeDtypeStruct((spots // SIDE + tag.shape[1], width), BF16)] * SIDE
    smem, vmem = (pl.BlockSpec(memory_space=m) for m in (pltpu.SMEM, pltpu.VMEM))
    return pl.pallas_call(
        combine_kernel,
        out_shape=out_shape,
        in_specs=[smem] + [vmem] * len(operands),
        out_specs=[pl.BlockSpec(memory_space=pl.ANY)] + [vmem] * SIDE,
        scratch_shapes=[
            pltpu.VMEM((2 * SIDE * part, width), BF16),
            pltpu.VMEM((2 * SIDE, part, width), F32),
            pltpu.SemaphoreType.DMA((2 * SIDE,)),
        ],
        compiler_params=pltpu.CompilerParams(vmem_limit_bytes=16 * 1024 * 1024),
        cost_estimate=pl.CostEstimate(
            flops=2 * spots * 2 * SIDE * part * width, bytes_accessed=1 << 22, transcendentals=0
        ),
    )(flags, *operands)


def halves(one, other, early, cut=2):
    def kernel(one, other, early, first, second, sems):
        half = first.shape[0]
        copies = [
            pltpu.make_async_copy(one.at[pl.ds(0, half)], first, sems.at[0]),
            pltpu.make_async_copy(other.at[pl.ds(other.shape[0] - half, half)], second, sems.at[1]),
        ]
        for copy in copies:
            copy.start()
        for copy in copies:
            copy.wait()

    shape = jax.ShapeDtypeStruct((one.shape[0] // cut,) + one.shape[1:], one.dtype)
    anywhere = pl.BlockSpec(memory_space=pl.ANY)
    return pl.pallas_call(
        kernel,
        out_shape=[shape, shape],
        in_specs=[anywhere] * 3,
        out_specs=[anywhere] * 2,
        scratch_shapes=[pltpu.SemaphoreType.DMA((2,))],
        compiler_params=pltpu.CompilerParams(vmem_limit_bytes=1024 * 1024),
        cost_estimate=pl.CostEstimate(
            flops=0, bytes_accessed=2 * one.size * 2, transcendentals=0
        ),
    )(one, other, early)


def first_kernel(order, rows, early, *refs, first, last, features):
    weights, refs = [refs[2 * b : 2 * b + 2] for b in range(PER)], refs[2 * PER :]
    routers, refs = refs[:PER], refs[PER:]
    gains, refs = refs[:PER], refs[PER:]
    carried = None
    if not first:
        carried, refs = refs[:3], refs[3:]
    if last:
        select, hidden, weight, acc, logits, squares = refs
    else:
        acc, logits, squares = refs

    @pl.when(pl.program_id(0) == 0)
    def _():
        for at, ref in enumerate((acc, logits, squares)):
            ref[...] = jnp.zeros_like(ref) if first else carried[at][...]

    scaled = []
    for b in range(PER):
        values = rows[b].astype(F32)
        square = values * values
        for lane in range(0, values.shape[1], 128):
            squares[...] += square[:, lane : lane + 128]
        scaled.append((values * gains[b][...]).astype(BF16))
    for at in range(2):
        for core in range(2):
            total = acc[2 * at + core]
            for b in range(PER):
                total += jnp.dot(scaled[b], weights[b][at][core], preferred_element_type=F32)
            acc[2 * at + core] = total
    total = logits[...]
    for b in range(PER):
        total += lax.dot_general(
            scaled[b], routers[b][...], (((1,), (1,)), ((), ())), preferred_element_type=F32
        )
    logits[...] = total

    if last:

        @pl.when(pl.program_id(0) == pl.num_programs(0) - 1)
        def _():
            mean = jnp.sum(squares[...], axis=1, keepdims=True) / features
            scale = lax.rsqrt(mean + 1e-06)
            gap = jnp.sum(logits[...] * select[...], axis=1, keepdims=True) * scale
            weight[...] = jnp.broadcast_to(1.0 / (1.0 + jnp.exp(-gap)), weight.shape)
            for core in range(2):
                gate = acc[core] * scale
                upper = acc[2 + core] * scale
                width = gate.shape[1]
                hidden[:, core * width : (core + 1) * width] = (
                    gate / (1.0 + jnp.exp(-gate)) * upper
                ).astype(BF16)


def first_products(rows, places, gate, up, router, gain, carried, select, early):
    blocks, count, depth = rows.shape
    features, width = gate.shape[1:]
    experts = router.shape[0]
    first, last = carried is None, select is not None
    whole = lambda *shape: pl.BlockSpec(shape, lambda i, order: (0,) * len(shape))

    def weight_spec(b):
        return pl.BlockSpec((2, depth, width), lambda i, order: (0, order[i * PER + b], 0))

    def flat_spec(b, height):
        return pl.BlockSpec((height, depth), lambda i, order: (0, order[i * PER + b]))

    in_specs = [
        pl.BlockSpec((PER, count, depth), lambda i, order: (i, 0, 0)),
        pl.BlockSpec((1, 8, 128), lambda i, order: (0, 0, 0)),
    ]
    operands = [rows, in_hbm(early)]
    for b in range(PER):
        in_specs += [weight_spec(b)] * 2
        operands += [in_hbm(gate), in_hbm(up)]
    in_specs += [flat_spec(b, experts) for b in range(PER)]
    operands += [router] * PER
    in_specs += [flat_spec(b, 1) for b in range(PER)]
    operands += [gain] * PER
    sums = [(4, count, width), (count, experts), (count, 128)]
    if not first:
        in_specs += [whole(*shape) for shape in sums]
        operands += list(carried)
    scratch = []
    if last:
        in_specs.append(whole(count, experts))
        operands.append(select)
        out_shape = [
            jax.ShapeDtypeStruct((count, 2 * width), BF16),
            jax.ShapeDtypeStruct((count, 128), F32),
        ]
        scratch = [pltpu.VMEM(shape, F32) for shape in sums]
    else:
        out_shape = [jax.ShapeDtypeStruct(shape, F32) for shape in sums]
    return pl.pallas_call(
        lambda *refs: first_kernel(*refs, first=first, last=last, features=features),
        out_shape=out_shape,
        grid_spec=pltpu.PrefetchScalarGridSpec(
            num_scalar_prefetch=1,
            grid=(blocks // PER,),
            in_specs=in_specs,
            out_specs=[whole(*s.shape) for s in out_shape],
            scratch_shapes=scratch,
        ),
        compiler_params=pltpu.CompilerParams(
            dimension_semantics=("arbitrary",), vmem_limit_bytes=VMEM
        ),
        cost_estimate=pl.CostEstimate(
            flops=2 * count * depth * blocks * width * 4,
            bytes_accessed=blocks * depth * width * 8,
            transcendentals=0,
        ),
    )(places, *operands)


def in_hbm(value):
    return pltpu.with_memory_space_constraint(value, pltpu.HBM)


def in_vmem(value):
    return pltpu.with_memory_space_constraint(value, pltpu.VMEM)


def products_kernel(order, *refs, pieces, distances, last, features):
    rows, refs = refs[:pieces], refs[pieces:]
    gate, up, router, gain, *refs = refs
    carried, refs = refs[:3], refs[3:]
    if last:
        select, hidden, weight = refs
    else:
        acc, logits, squares = refs
    count, depth = rows[0].shape[1:]
    width = gate.shape[2]
    scaled, spans = [], []
    square_sum = carried[2][...]
    arrived = [(ref, at) for ref in rows for at in range(ref.shape[0])]
    for b, (ref, at) in enumerate(arrived):
        block = order[distances[b // SIDE] * SIDE + b % SIDE]
        span = pl.ds(pl.multiple_of(block * depth, depth), depth)
        values = ref[at].astype(F32)
        square = values * values
        for lane in range(0, depth, 128):
            square_sum += square[:, lane : lane + 128]
        scaled.append((values * gain[:, span]).astype(BF16))
        spans.append(span)
    totals = []
    for at, matrix in enumerate((gate, up)):
        for core in range(2):
            total = carried[0][2 * at + core]
            for values, span in zip(scaled, spans):
                total += jnp.dot(values, matrix[core, span, :], preferred_element_type=F32)
            if last:
                totals.append(total)
            else:
                acc[2 * at + core] = total
    total = carried[1][...]
    for values, span in zip(scaled, spans):
        total += lax.dot_general(
            values, router[:, span], (((1,), (1,)), ((), ())), preferred_element_type=F32
        )
    if not last:
        logits[...] = total
        squares[...] = square_sum
        return
    mean = jnp.sum(square_sum, axis=1, keepdims=True) / features
    scale = lax.rsqrt(mean + 1e-06)
    gap = jnp.sum(total * select[...], axis=1, keepdims=True) * scale
    weight[...] = jnp.broadcast_to(1.0 / (1.0 + jnp.exp(-gap)), weight.shape)
    for core in range(2):
        gated = totals[core] * scale
        upper = totals[2 + core] * scale
        hidden[:, core * width : (core + 1) * width] = (
            gated / (1.0 + jnp.exp(-gated)) * upper
        ).astype(BF16)


def local_call(kernel, places, operands, out_shape, flops, touched):
    smem, vmem = (pl.BlockSpec(memory_space=m) for m in (pltpu.SMEM, pltpu.VMEM))
    return pl.pallas_call(
        kernel,
        out_shape=out_shape,
        in_specs=[smem] + [vmem] * len(operands),
        out_specs=jax.tree.map(lambda _: vmem, out_shape),
        compiler_params=pltpu.CompilerParams(vmem_limit_bytes=VMEM),
        cost_estimate=pl.CostEstimate(flops=flops, bytes_accessed=touched, transcendentals=0),
    )(places, *operands)


def products(rows, places, distances, gate, up, router, gain, carried, select):
    count, depth = rows[0].shape[1:]
    blocks = SIDE * len(distances)
    features, width = gate.shape[1:]
    last = select is not None
    operands = [*rows, in_vmem(gate), in_vmem(up), router, gain, *map(in_vmem, carried)]
    if last:
        operands.append(select)
        out_shape = [
            jax.ShapeDtypeStruct((count, 2 * width), BF16),
            jax.ShapeDtypeStruct((count, 128), F32),
        ]
    else:
        sums = [(4, count, width), (count, router.shape[0]), (count, 128)]
        out_shape = [jax.ShapeDtypeStruct(shape, F32) for shape in sums]
    return local_call(
        lambda *refs: products_kernel(
            *refs, pieces=len(rows), distances=distances, last=last, features=features
        ),
        places,
        operands,
        out_shape,
        2 * count * depth * blocks * width * 4,
        blocks * depth * width * 8,
    )


def down_kernel(order, hidden, weight, down, out, *, distance, start):
    width, depth = hidden.shape[1] // 2, out.shape[2]
    for b in range(out.shape[0]):
        block = order[distance * SIDE + start + b]
        span = pl.ds(pl.multiple_of(block * depth, depth), depth)
        term = jnp.dot(hidden[:, :width], down[0, :, span], preferred_element_type=F32)
        term += jnp.dot(hidden[:, width:], down[1, :, span], preferred_element_type=F32)
        out[b] = (term * weight[:, :1]).astype(BF16)


def down_terms(hidden, weight, places, distance, down, depth, start=0, blocks=SIDE):
    count, both = hidden.shape
    return local_call(
        functools.partial(down_kernel, distance=distance, start=start),
        places,
        [hidden, weight, in_vmem(down)],
        jax.ShapeDtypeStruct((blocks, count, depth), BF16),
        2 * count * both * depth * blocks,
        both * depth * blocks * 2,
    )


def body(
    mixer_out,
    out_proj,
    residual,
    norm_gain,
    router_weight,
    expert_ids,
    expert_gate,
    expert_up,
    expert_down,
):
    node = lax.axis_index("node")
    local = lax.axis_index("local")
    core = lax.axis_index("tp")
    x, y = local // SIDE, local % SIDE
    half_rows, col_width = residual.shape
    capacity = half_rows // 16
    spots = SIDE * capacity
    part = mixer_out.shape[0]

    gate, up, down = (
        lax.all_gather(w, "tp", axis=0, tiled=True) for w in (expert_gate, expert_up, expert_down)
    )

    first, partner = expert_ids[:, 0], expert_ids[:, 1]
    routed = first < SIDE
    relative = lax.rem(first - node + SIDE, SIDE)
    marks = (routed[:, None] & (relative[:, None] == jnp.arange(SIDE)[None, :])).astype(jnp.int32)
    slots = jnp.sum((jnp.cumsum(marks, axis=0) - marks) * marks, axis=1)
    spot = jnp.where(routed, relative * capacity + slots, -1)
    placed = (spot[:, None] == jnp.arange(spots)[None, :]).astype(BF16)
    picked = spot[None, :] == jnp.arange(spots)[:, None]
    partners = jnp.sum(jnp.where(picked, partner[None, :], 0), axis=1).reshape(SIDE, capacity)
    mine = [((x + p) % SIDE) // 2 == core for p in range(2)]

    flags = [core == 0] + mine + [(x + p) % 2 for p in range(2)] + [(y + dy) % SIDE for dy in range(SIDE)]
    flags = jnp.stack([f.astype(jnp.int32) for f in flags])

    ahead, behind = shift_mixed(mixer_out, False, -1), shift_mixed(mixer_out, False, 1)
    across = [
        shift_mixed(behind[: part // 2], False, 1),
        shift_mixed(ahead[part // 2 :], False, -1),
    ]
    low = jnp.concatenate([mixer_out, ahead], axis=0)
    low_1, low_3 = shift_mixed(low, True, -1), shift_mixed(low, True, 1)
    high = jnp.concatenate(across + [behind], axis=0)
    high_1, high_3 = shift_mixed(high, True, -1), shift_mixed(high, True, 1)
    far_2 = []
    for behind, ahead in ((low_3, low_1), (high_3, high_1)):
        first_half, second_half = halves(behind, ahead, flags)
        far_2 += [shift_mixed(first_half, True, 1), shift_mixed(second_half, True, -1)]

    def project(rows):
        return lax.optimization_barrier(jnp.dot(rows, out_proj, preferred_element_type=F32))

    lows = {far: project(rows) for far, rows in ((0, low), (1, low_1), (3, low_3))}
    highs = {far: project(rows) for far, rows in ((0, high), (1, high_1), (3, high_3))}
    lasts = [project(rows) for rows in far_2]

    def block(far, near):
        if far == 2:
            return lasts[near]
        half = (lows if near < 2 else highs)[far]
        return half[near % 2 * part : (near % 2 + 1) * part]

    def sent(names_0, names_1):
        out = []
        for (p, dy), (q, ey) in zip(names_0, names_1):
            along_x = jnp.where(mine[p], block(dy, p + 2), block(dy, p))
            along_y = jnp.where(mine[q], block(q + 2, ey), block(q, ey))
            out.append(jnp.where(core == 0, along_x, along_y))
        return jnp.stack(out).astype(BF16)

    got_early, got_late = swap_core(sent(EARLY_0, EARLY_1)), swap_core(sent(LATE_0, LATE_1))
    tag = jnp.zeros((SIDE, 16, col_width), BF16).at[:, 0, :capacity].set(partners.astype(BF16))
    stream, *bucket = combine(
        flags,
        [lows[far] for far in (0, 1, 3)],
        [highs[far] for far in (0, 1, 3)],
        lasts,
        got_early,
        got_late,
        residual.reshape(2 * SIDE, part, col_width),
        picked.astype(BF16),
        tag,
    )
    stream = stream.reshape(half_rows, col_width)

    landed = [bucket[0]] + [shift_node(bucket[d], d) for d in (1, 3, 2)]
    partners = jnp.concatenate([v[capacity, :capacity] for v in landed]).astype(jnp.int32)
    landed = jnp.concatenate([v[:capacity] for v in landed], axis=0)
    experts = jnp.arange(router_weight.shape[1])[None, :]
    select = (experts == node).astype(F32) - (experts == partners[:, None]).astype(F32)
    got = {(-d) % SIDE: shift_mixed(landed, False, d) for d in (1, 3, 2)}
    line_a, line_b = jnp.stack([landed, got[1]]), jnp.stack([got[2], got[3]])
    behind_a, ahead_b = shift_mixed(line_a, True, 1), shift_mixed(line_b, True, -1)
    behind_b, ahead_a = shift_mixed(line_b, True, 1), shift_mixed(line_a, True, -1)
    line = jnp.concatenate([line_a, line_b], axis=0)
    ring_x = ((x + jnp.arange(SIDE)) % SIDE) * SIDE
    ring_y = (y + jnp.arange(SIDE)) % SIDE
    order = jnp.where(
        core == 0, ring_x[None, :] + ring_y[:, None], ring_x[:, None] + ring_y[None, :]
    )
    order = order.reshape(-1).astype(jnp.int32)

    carried = first_products(
        line, order, gate, up, router_weight.T, norm_gain[None, :], None, None, down
    )
    first_half, second_half = halves(behind_a, ahead_b, carried[1], 1)
    across = [shift_mixed(first_half, True, 1), shift_mixed(second_half, True, -1)]
    for stage in ((1, 3), (2,)):
        carried = products(
            [ahead_a, ahead_b, behind_a, behind_b] if stage == (1, 3) else across,
            order,
            stage,
            gate,
            up,
            router_weight.T,
            norm_gain[None, :],
            carried,
            select if stage == (2,) else None,
        )
    hidden, weight = carried

    low, high = (
        down_terms(hidden, weight, order, 2, down, col_width, start, 2) for start in (0, 2)
    )
    low, high = shift_mixed(low, True, 1), shift_mixed(high, True, -1)
    one, three, zero = (
        down_terms(hidden, weight, order, d, down, col_width) for d in (1, 3, 0)
    )
    none = jnp.zeros_like(low)
    one = one.astype(F32) + jnp.concatenate([low, none], axis=0).astype(F32)
    three = three.astype(F32) + jnp.concatenate([none, high], axis=0).astype(F32)
    got = shift_mixed(one.astype(BF16), True, 1), shift_mixed(three.astype(BF16), True, -1)
    line = sum((g.astype(F32) for g in got), zero.astype(F32)).astype(BF16)
    got = [shift_mixed(line[d], False, d) for d in (1, 3, 2)]
    summed = sum((g.astype(F32) for g in got), line[0].astype(F32)).astype(BF16)
    summed = summed.reshape(SIDE, capacity, col_width)
    back = {d: shift_node(summed[at], -d) for at, d in ((1, 1), (2, 3), (3, 2))}
    returned = jnp.concatenate([summed[0]] + [back[d] for d in range(1, SIDE)], axis=0)
    expert_sum = jnp.dot(placed, returned, preferred_element_type=F32)
    return (stream + expert_sum).astype(BF16)


def solution(mesh):
    placed = (
        P(("node", "local"), "tp"),
        P("tp", "local"),
        P(("node", "tp"), "local"),
        P(),
        P(),
        P(("node", "tp"), None),
        P("node", None, ("local", "tp")),
        P("node", None, ("local", "tp")),
        P("node", ("local", "tp"), None),
    )
    return jax.shard_map(
        body, mesh=mesh, in_specs=placed, out_specs=P(("node", "tp"), "local"), check_vma=False
    )
```
